32 devices in a mesh: row: 4 (over y, x), col: 8 (over z, core).
Axes of the slice: x: 2, y: 2, z: 4, core: 2. Of those that a mesh axis runs over, the one named last changes fastest.
Arguments:
- a_blocks: bfloat16 [8, 4, 16, 32, 128], P('col', 'row'), may hold values from -1 to 1
- a_scale: float32 [8, 4, 16, 4], P('col', 'row'), may hold values from 0.25 to 4
- a_cols: int32 [8, 4, 16, 4], P('col', 'row'), may hold values from 0 to 1023, as said below
- b_blocks: bfloat16 [8, 4, 1024, 32, 128], P('col', 'row'), may hold values from -1 to 1
- b_scale: float32 [8, 4, 1024, 4], P('col', 'row'), may hold values from 0.25 to 4
- b_cols: int32 [8, 4, 1024, 4], P('col', 'row'), may hold values from 0 to 511, as said below
Outputs:
- product: bfloat16 [8, 4, 8, 32, 16384], P('col', 'row')
The draws below stay inside these ranges and needn't reach their ends.
Inputs may be any that keep to these rules, and one draw needn't show every extreme that they name: `a_cols`: the 4 columns of each block row are distinct. `b_cols`: the 4 columns of each block row are distinct.
All inputs are finite; a program needn't handle non-finite values.
Results may differ from the reference program's by a relative error of at most 0.0034.
Values may be sent and summed in bfloat16 or wider, within the bound.
No kernel may reach another device: no remote copies, remote signals or barrier semaphores. Data moves between devices by JAX's collectives and lax.ppermute only.
A program may use at most 192 MiB of HBM per device.

```python
import math
import jax
import jax.numpy as jnp
from jax import lax

BS = 32
ROWS = 16
JW = 512
RA = 4
RB = 4
KW = 1024
N_ROW = 4
N_COL = 8


def distinct_columns(key, count, limit, picks):
    scores = jax.random.randint(key, (count, limit), 0, 1 << 20) * limit + jnp.arange(limit, dtype=jnp.int32)
    return lax.top_k(scores, picks)[1].astype(jnp.int32)


def draw_a_cols(key, part):
    picked = distinct_columns(jax.random.fold_in(key, 11), N_COL * N_ROW * ROWS, KW, RA)
    return picked.reshape(N_COL, N_ROW, ROWS, RA)


def draw_b_cols(key, part):
    picked = distinct_columns(jax.random.fold_in(key, 23), N_COL * N_ROW * KW, JW, RB)
    return picked.reshape(N_COL, N_ROW, KW, RB)


def steps_of(key, shape, shards, least, largest):
    def one(position, shards_of):
        draws = jax.random.uniform(jax.random.fold_in(jax.random.fold_in(key, 6), position), (shards_of,), jnp.float32, least / len(shards), largest / len(shards))
        return jnp.repeat(jnp.exp(draws), shape[position] // shards_of).reshape((-1,) + (1,) * (len(shape) - position - 1))

    loudness = one(*shards[0])
    for cut in shards[1:]:
        loudness = loudness * one(*cut)
    return loudness


def gaussian(stream_key, shape, width, most, pieces=(), kind=jnp.bfloat16):
    drawn = jax.random.normal(stream_key, shape, jnp.float32) * width
    if len(pieces) > 0:
        drawn = steps_of(stream_key, shape, pieces, -0.22, 0.18) * drawn
    return jnp.clip(drawn, min=-most, max=most).astype(kind)


def setup_inputs(seed: int = 0) -> dict:
    streams_of = jax.random.split(jax.random.key(seed), 7)
    return {
        "a_blocks": gaussian(streams_of[0], (N_COL, N_ROW, ROWS, BS, RA * BS), 0.125, 1.0, ((0, 8), (1, 4))),
        "a_scale": jnp.clip(jnp.exp(math.log(4.0) - 2.7725887 * jax.random.uniform(streams_of[1], (N_COL, N_ROW, ROWS, RA), jnp.float32) ** steps_of(streams_of[1], (N_COL, N_ROW, ROWS, RA), ((0, 8), (1, 4)), -0.2, 0.2)), 0.25, 4.0),
        "a_cols": draw_a_cols(jax.random.fold_in(streams_of[6], 71), 0),
        "b_blocks": gaussian(streams_of[3], (N_COL, N_ROW, KW, BS, RB * BS), 0.125, 1.0, ((0, 8), (1, 4))),
        "b_scale": jnp.clip(jnp.exp(math.log(4.0) - 2.7725887 * jax.random.uniform(streams_of[4], (N_COL, N_ROW, KW, RB), jnp.float32) ** steps_of(streams_of[4], (N_COL, N_ROW, KW, RB), ((0, 8), (1, 4)), -0.2, 0.2)), 0.25, 4.0),
        "b_cols": draw_b_cols(jax.random.fold_in(streams_of[6], 71), 0),
    }


def block_sum(total, a_part, a_scl, a_idx, b_part, b_scl, b_idx):
    nrows, bsize, _ = a_part.shape
    slots_a = a_scl.shape[1]
    slots_b = b_scl.shape[1]
    left = a_part.reshape(nrows, bsize, slots_a, bsize).astype(jnp.float32)
    right = jnp.take(b_part, a_idx, axis=0).astype(jnp.float32)
    right_scl = jnp.take(b_scl, a_idx, axis=0)
    right_idx = jnp.take(b_idx, a_idx, axis=0)
    prods = lax.dot_general(left, right, (((3,), (2,)), ((0, 2), (0, 1))), precision=lax.Precision.HIGHEST, preferred_element_type=jnp.float32)
    prods = prods.reshape(nrows, slots_a, bsize, slots_b, bsize)
    prods = jnp.transpose(prods, (0, 1, 3, 2, 4))
    scaled = prods * (a_scl[:, :, None] * right_scl)[..., None, None]
    scaled = scaled.reshape(nrows, slots_a, slots_b, bsize * bsize)
    row_ids = jnp.broadcast_to(jnp.arange(nrows, dtype=jnp.int32)[:, None, None], right_idx.shape)
    return total.at[row_ids, right_idx].add(scaled)


def reference(a_blocks, a_scale, a_cols, b_blocks, b_scale, b_cols):
    panels = N_ROW

    def one_panel(index):
        owner = index // panels
        target = index % panels

        def partial_value(half):
            def tick(inner, total):
                a_at = (inner - owner) % panels
                b_at = 2 * ((inner - target) % panels) + half
                a_row = 2 * owner + half
                return block_sum(total, a_blocks[a_row, a_at], a_scale[a_row, a_at], a_cols[a_row, a_at], b_blocks[b_at, target], b_scale[b_at, target], b_cols[b_at, target])

            start = jnp.zeros((ROWS, JW, BS * BS), jnp.float32)
            summed = lax.fori_loop(0, panels, tick, start)
            return lax.optimization_barrier(summed.astype(jnp.bfloat16)).astype(jnp.float32)

        whole = (partial_value(0) + partial_value(1)).astype(jnp.bfloat16)
        whole = whole.reshape(ROWS, JW, BS, BS)
        return jnp.transpose(whole, (0, 2, 1, 3)).reshape(ROWS, BS, JW * BS)

    every = lax.map(one_panel, jnp.arange(panels * panels, dtype=jnp.int32))
    every = every.reshape(panels, panels, 2, ROWS // 2, BS, JW * BS)
    every = jnp.transpose(every, (0, 2, 1, 3, 4, 5))
    return every.reshape(2 * panels, panels, ROWS // 2, BS, JW * BS)
```

```python
import functools

import jax
import jax.numpy as jnp
from jax import lax
from jax.experimental import pallas as pl
from jax.experimental.pallas import tpu as pltpu
from jax.sharding import PartitionSpec as P

JW = 512
LANES = 128
META = 16
PARTS = 5
F32, BF16, I32 = jnp.float32, jnp.bfloat16, jnp.int32
VMEM_LIMIT = 12 * 1024 * 1024


def in_vmem(x):
    return pltpu.with_memory_space_constraint(x, pltpu.VMEM)


def three_parts(x):
    high = x.astype(BF16).astype(F32)
    rest = x - high
    mid = rest.astype(BF16).astype(F32)
    return [high, mid, (rest - mid).astype(BF16).astype(F32)]


def stacked(parts, rows):
    which = lax.broadcasted_iota(I32, (rows, parts[0].shape[1]), 0)
    tile = jnp.zeros(which.shape, F32)
    for at, part in enumerate(parts):
        tile = jnp.where(which == at, jnp.broadcast_to(part, which.shape), tile)
    return tile


def entries(values, first, half, rb):
    ra = values.shape[0]
    one = [values[m : m + 1, first : first + half] for m in range(ra)]
    return jnp.concatenate(one * rb, axis=1)


def gather_kernel(half, ra, rb, bs, first, pieces, cuts, *refs):
    refs = list(refs)
    take = lambda count: [refs.pop(0) for _ in range(count)]
    parity, cols_s, cols_v, b = take(4)
    if first:
        bscale, bcols = take(2)
    else:
        (table,) = take(1)
    if pieces:
        a, ascale = take(2)
    (b_same,) = take(1)
    if first:
        table, acc = take(2)
    if pieces:
        halves_of_a = take(2)
    outs = [take(len(cut)) for cut in cuts]
    wide = ra * bs
    kw = b.shape[0]
    odd = parity[0] == 1

    for flip in range(2):
        base = (parity[0] ^ flip) * half
        for out, (start, stop) in zip(outs[flip], cuts[flip]):

            def one_row(i, _, out=out, start=start, base=base):
                for m in range(ra):
                    t = cols_s[m, base + i]
                    at = pl.multiple_of(((i - start) * ra + m) * bs, bs)
                    out[pl.ds(at, bs), :] = b[t]
                return 0

            lax.fori_loop(start, stop, one_row, 0, unroll=2)

    if first:
        scale, column = bscale[...], bcols[...]
        rows = three_parts(scale) + [(column >> 8).astype(F32), (column & 255).astype(F32)]
        rows.append(jnp.zeros((table.shape[0] - PARTS * rb, kw), F32))
        table[...] = jnp.concatenate(rows, axis=0).astype(BF16)

    cols = cols_v[...]
    both = [entries(cols, h * half, half, rb) for h in range(2)]
    for flip in range(2):
        named = jnp.where(odd != (flip == 1), both[1], both[0])
        named = jnp.broadcast_to(named, (kw, named.shape[1]))
        picked = lax.broadcasted_iota(I32, named.shape, 0) == named
        picked = jnp.where(picked, 1.0, 0.0).astype(BF16)
        found = jnp.dot(table[...], picked, preferred_element_type=F32)
        slot = lax.broadcasted_iota(I32, (1, found.shape[1]), 1) // (ra * half)
        parts = []
        for part in range(PARTS):
            value = found[part * rb : part * rb + 1]
            for n in range(1, rb):
                value = jnp.where(slot == n, found[part * rb + n : part * rb + n + 1], value)
            parts.append(value)
        tile = stacked(parts, META).astype(BF16)
        for out, (start, stop) in zip(outs[flip], cuts[flip]):
            out[pl.ds((stop - start) * wide, META), :] = tile

    if pieces:
        scale = ascale[...]
        both = [entries(scale, h * half, half, rb) for h in range(2)]
        for flip, out in enumerate(halves_of_a):
            base = (parity[0] ^ flip) * half
            out[pl.ds(0, half * bs), :] = a[pl.ds(pl.multiple_of(base * bs, bs), half * bs), :]
            parts = three_parts(jnp.where(odd != (flip == 1), both[1], both[0]))
            out[pl.ds(half * bs, META), :] = stacked(parts, META).astype(BF16)

    if first:
        tiles = acc.shape[1]
        for i in range(acc.shape[0]):

            def clear(tile, _, i=i):
                acc[i, tile] = jnp.zeros(acc.shape[2:], F32)
                return 0

            lax.fori_loop(0, tiles, clear, 0, unroll=8)


def gather(parity, cols, b, half, cuts, tables=None, table=None, a=None):
    ra = cols.shape[0]
    kw, bs, width = b.shape
    rb = width // bs
    first = table is None
    smem, vmem = pl.BlockSpec(memory_space=pltpu.SMEM), pl.BlockSpec(memory_space=pltpu.VMEM)
    args = [parity, cols, cols, in_vmem(b)]
    specs = [smem, smem, vmem, vmem]
    outs = [pltpu.VMEM(b.shape, BF16)]
    if first:
        args += tables
        tiles = JW * bs // LANES
        outs.append(pltpu.VMEM((32, kw), BF16))
        outs.append(pltpu.VMEM((half, tiles, bs, LANES), F32))
    else:
        args.append(in_vmem(table))
    if a is not None:
        args += a
        outs += [pltpu.VMEM((half * bs + META, ra * bs), BF16)] * 2
    for cut in cuts:
        for start, stop in cut:
            outs.append(pltpu.VMEM(((stop - start) * ra * bs + META, width), BF16))
    specs += [vmem] * (len(args) - len(specs))
    got = pl.pallas_call(
        functools.partial(gather_kernel, half, ra, rb, bs, first, a is not None, cuts),
        out_shape=outs,
        in_specs=specs,
        out_specs=[vmem] * len(outs),
        input_output_aliases={3: 0},
        compiler_params=pltpu.CompilerParams(vmem_limit_bytes=VMEM_LIMIT),
        cost_estimate=pl.CostEstimate(flops=0, bytes_accessed=4 * 2**20, transcendentals=0),
        name="gather_rows",
    )(*args)
    got = list(got)
    messages = [[got.pop() for _ in cut][::-1] for cut in cuts[::-1]][::-1]
    return got, messages


def add_kernel(ra, rb, bs, flip, rows, flush, has_out, *refs):
    refs = list(refs)
    a, b, _ = refs.pop(0), refs.pop(0), refs.pop(0)
    if has_out:
        refs.pop(0)
    acc = refs.pop(0)
    if flush:
        target = refs.pop(0)
    prod, scl_v, col_v, scl_s, col_s, stage, sems, out_sems = refs
    first, last = rows
    wide = ra * bs
    half, tiles = acc.shape[:2]
    per = LANES // bs
    a_meta = a[flip, pl.ds(a.shape[1] - META, META), :].astype(F32)
    b_meta = b[pl.ds(b.shape[0] - META, META), :].astype(F32)
    scl_a = a_meta[0:1] + a_meta[1:2] + a_meta[2:3]
    scl_b = b_meta[0:1] + b_meta[1:2] + b_meta[2:3]
    scl_v[...] = jnp.broadcast_to(scl_a * scl_b, scl_v.shape)
    col_v[...] = jnp.broadcast_to((b_meta[3:4] * 256.0 + b_meta[4:5]).astype(I32), col_v.shape)
    moves = [
        pltpu.make_async_copy(scl_v, scl_s, sems.at[0]),
        pltpu.make_async_copy(col_v, col_s, sems.at[1]),
    ]
    for move in moves:
        move.start()
    row_block = lax.broadcasted_iota(I32, (wide, wide), 0) // bs
    col_block = lax.broadcasted_iota(I32, (wide, wide), 1) // bs
    diagonal = jnp.where(row_block == col_block, 1.0, 0.0).astype(BF16)
    for i in range(first, last):
        left = a[flip, pl.ds(i * bs, bs), :]
        left = jnp.concatenate([left] * ra, axis=0) * diagonal
        right = b[pl.ds((i - first) * wide, wide), :]
        prod[pl.ds((i - first) * wide, wide), :] = jnp.dot(left, right, preferred_element_type=F32)
    for move in moves:
        move.wait()
    lane_block = lax.broadcasted_iota(I32, (bs, LANES), 1) // bs

    def one_row(i, _):
        for m in range(ra):
            value = prod[pl.ds(pl.multiple_of(((i - first) * ra + m) * bs, bs), bs), :]
            for n in range(rb):
                entry = (n * ra + m) * half + i
                column = col_s[0, entry]
                place = column & (per - 1)
                moved = pltpu.roll(value, ((place - n) & (per - 1)) * bs, 1)
                moved = jnp.where(lane_block == place, moved * scl_s[0, entry], 0.0)
                tile = column // per
                acc[i, tile] = acc[i, tile] + moved
        return 0

    lax.fori_loop(first, last, one_row, 0)
    if flush:

        def send(i):
            slot = (i - first) % 2
            return pltpu.make_async_copy(stage.at[slot], target.at[i], out_sems.at[slot])

        for i in range(first, last):
            if i - first >= 2:
                send(i - 2).wait()
            for tile in range(tiles):
                stage[(i - first) % 2, :, pl.ds(tile * LANES, LANES)] = acc[i, tile].astype(BF16)
            send(i).start()
        for i in range(max(first, last - 2), last):
            send(i).wait()


def add_products(a, b, flip, shape, rows, acc, flush=False, out=None):
    half, ra, rb, bs = shape
    out_shapes = [pltpu.VMEM(acc.shape, F32)]
    if flush:
        out_shapes.append(jax.ShapeDtypeStruct((half, bs, JW * bs), BF16))
    vmem = pl.BlockSpec(memory_space=pltpu.VMEM)
    anywhere = pl.BlockSpec(memory_space=pl.ANY)
    args, specs = [a, b, in_vmem(acc)], [vmem] * 3
    aliases = {2: 0}
    if out is not None:
        aliases[len(args)] = 1
        args.append(out)
        specs.append(anywhere)
    count = rows[1] - rows[0]
    return pl.pallas_call(
        functools.partial(add_kernel, ra, rb, bs, flip, rows, flush, out is not None),
        out_shape=out_shapes,
        in_specs=specs,
        out_specs=[vmem, anywhere][: len(out_shapes)],
        input_output_aliases=aliases,
        scratch_shapes=[
            pltpu.VMEM((count * ra * bs, rb * bs), F32),
            pltpu.VMEM((8, LANES), F32),
            pltpu.VMEM((8, LANES), I32),
            pltpu.SMEM((8, LANES), F32),
            pltpu.SMEM((8, LANES), I32),
            pltpu.VMEM((2, bs, JW * bs) if flush else (2, 16, LANES), BF16),
            pltpu.SemaphoreType.DMA((2,)),
            pltpu.SemaphoreType.DMA((2,)),
        ],
        compiler_params=pltpu.CompilerParams(vmem_limit_bytes=VMEM_LIMIT),
        cost_estimate=pl.CostEstimate(flops=0, bytes_accessed=6 * 2**20, transcendentals=0),
        name="add_products",
    )(*args)


def on_device(a_blocks, a_scale, a_cols, b_blocks, b_scale, b_cols):
    panels = lax.axis_size("row")
    columns = lax.axis_size("col")
    halves = columns // panels
    a_part, a_scl, a_pos = a_blocks[0, 0], a_scale[0, 0].T, a_cols[0, 0].T
    b_part = b_blocks[0, 0]
    b_scl, b_pos = b_scale[0, 0].T, b_cols[0, 0].T
    nrows, bs, _ = a_part.shape
    ra, rb = a_scl.shape[0], b_scl.shape[0]
    half = nrows // halves
    shape = (half, ra, rb, bs)
    parity = (lax.axis_index("col") % halves).astype(I32).reshape(1)

    def step(value, by, flip):
        pairs = [
            (c, ((c // halves + by) % panels) * halves + (c % halves ^ flip)) for c in range(columns)
        ]
        return lax.ppermute(value, "col", pairs)

    def named_by(by):
        pairs = []
        for r in range(panels):
            for c in range(columns):
                to_row = (r + by) % panels
                to_col = (c - halves * by) % columns
                pairs.append((r * columns + c, to_row * columns + to_col))
        return lax.ppermute(a_pos, ("row", "col"), pairs)

    order = sorted(range(1, panels), key=lambda by: -min(by, panels - by))
    asked = {by: named_by(by) for by in order}
    every = (0, half)
    early = (0, half - max(1, half // 4))
    late = (early[1], half)

    messages = {}
    (b_here, table, acc), messages[0] = gather(
        parity, a_pos, b_part, half, [[every], [every]], tables=[b_scl, b_pos]
    )
    for place, by in enumerate(order):
        a = [a_part.reshape(nrows * bs, ra * bs), a_scl] if place == min(1, len(order) - 1) else None
        cuts = [[every], [early, late] if by == order[-1] else [every]]
        got, messages[by] = gather(parity, asked[by], b_here, half, cuts, table=table, a=a)
        b_here = got[0]
        if a is not None:
            kept, given = got[1:]
    left = {0: jnp.stack([kept, step(given, 0, 1)])}
    for by in order:
        pairs = [(r, (r + by) % panels) for r in range(panels)]
        left[by] = lax.ppermute(left[0], "row", pairs)

    (acc,) = add_products(kept[None], messages[0][0][0], 0, shape, every, acc)
    (acc,) = add_products(left[0], step(messages[0][1][0], 0, 1), 1, shape, every, acc)
    for by in order:
        for flip in range(halves):
            arrived = [step(message, by, flip) for message in messages[by][flip]]
            if len(arrived) == 1:
                (acc,) = add_products(left[by], arrived[0], flip, shape, every, acc)
            else:
                acc, out = add_products(left[by], arrived[0], flip, shape, early, acc, flush=True)
                _, out = add_products(left[by], arrived[1], flip, shape, late, acc, flush=True, out=out)
    return out[None, None]


def solution(mesh):
    in_specs = (
        P("col", "row", None, None, None),
        P("col", "row", None, None),
        P("col", "row", None, None),
        P("col", "row", None, None, None),
        P("col", "row", None, None),
        P("col", "row", None, None),
    )
    out_specs = P("col", "row", None, None, None)
    return jax.shard_map(
        on_device, mesh=mesh, in_specs=in_specs, out_specs=out_specs, check_vma=False
    )
```

```python
import functools

import jax
import jax.numpy as jnp
from jax import lax
from jax.experimental import pallas as pl
from jax.experimental.pallas import tpu as pltpu
from jax.sharding import PartitionSpec as P

JW = 512
LANES = 128
META = 16
PARTS = 5
F32, BF16, I32 = jnp.float32, jnp.bfloat16, jnp.int32
VMEM_LIMIT = 12 * 1024 * 1024


def in_vmem(x):
    return pltpu.with_memory_space_constraint(x, pltpu.VMEM)


def three_parts(x):
    high = x.astype(BF16).astype(F32)
    rest = x - high
    mid = rest.astype(BF16).astype(F32)
    return [high, mid, (rest - mid).astype(BF16).astype(F32)]


def stacked(parts, rows):
    which = lax.broadcasted_iota(I32, (rows, parts[0].shape[1]), 0)
    tile = jnp.zeros(which.shape, F32)
    for at, part in enumerate(parts):
        tile = jnp.where(which == at, jnp.broadcast_to(part, which.shape), tile)
    return tile


def entries(values, first, half, rb):
    ra = values.shape[0]
    one = [values[m : m + 1, first : first + half] for m in range(ra)]
    return jnp.concatenate(one * rb, axis=1)


def prepare_kernel(rb, bscale, bcols, table, acc):
    scale, column = bscale[...], bcols[...]
    rows = three_parts(scale) + [(column >> 8).astype(F32), (column & 255).astype(F32)]
    rows.append(jnp.zeros((table.shape[0] - PARTS * rb, table.shape[1]), F32))
    table[...] = jnp.concatenate(rows, axis=0).astype(BF16)
    for i in range(acc.shape[0]):

        def clear(tile, _, i=i):
            acc[i, tile] = jnp.zeros(acc.shape[2:], F32)
            return 0

        lax.fori_loop(0, acc.shape[1], clear, 0, unroll=8)


def prepare(bscale, bcols, half, bs):
    rb, kw = bscale.shape
    vmem = pl.BlockSpec(memory_space=pltpu.VMEM)
    return pl.pallas_call(
        functools.partial(prepare_kernel, rb),
        out_shape=[
            pltpu.VMEM((-(-PARTS * rb // 16) * 16, kw), BF16),
            pltpu.VMEM((half, JW * bs // LANES, bs, LANES), F32),
        ],
        in_specs=[vmem] * 2,
        out_specs=[vmem] * 2,
        compiler_params=pltpu.CompilerParams(vmem_limit_bytes=VMEM_LIMIT),
        cost_estimate=pl.CostEstimate(flops=0, bytes_accessed=8 * 2**20, transcendentals=0),
        name="prepare",
    )(bscale, bcols)


def split_kernel(half, rb, bs, parity, a, ascale, after, kept, given):
    scale = ascale[...]
    both = [entries(scale, h * half, half, rb) for h in range(2)]
    odd = parity[0] == 1
    for flip, out in enumerate((kept, given)):
        base = (parity[0] ^ flip) * half
        out[pl.ds(0, half * bs), :] = a[pl.ds(pl.multiple_of(base * bs, bs), half * bs), :]
        parts = three_parts(jnp.where(odd != (flip == 1), both[1], both[0]))
        out[pl.ds(half * bs, META), :] = stacked(parts, META).astype(BF16)


def split(parity, a, ascale, half, rb, bs, after):
    smem, vmem = pl.BlockSpec(memory_space=pltpu.SMEM), pl.BlockSpec(memory_space=pltpu.VMEM)
    return pl.pallas_call(
        functools.partial(split_kernel, half, rb, bs),
        out_shape=[pltpu.VMEM((half * bs + META, a.shape[1]), BF16)] * 2,
        in_specs=[smem, vmem, vmem, pl.BlockSpec(memory_space=pl.ANY)],
        out_specs=[vmem] * 2,
        compiler_params=pltpu.CompilerParams(vmem_limit_bytes=VMEM_LIMIT),
        cost_estimate=pl.CostEstimate(flops=0, bytes_accessed=1024, transcendentals=0),
        name="split",
    )(parity, a, ascale, after)


def gather_kernel(half, ra, rb, bs, cuts, afters, parity, cols_s, cols_v, table, b, *refs):
    refs = list(refs)[afters:]
    outs = [[refs.pop(0) for _ in cut] for cut in cuts]
    (sems,) = refs
    wide = ra * bs
    kw = b.shape[0]
    odd = parity[0] == 1

    waits = []
    for flip in range(2):
        base = (parity[0] ^ flip) * half
        for out, (start, stop) in zip(outs[flip], cuts[flip]):
            sem = sems.at[len(waits)]

            def one_row(i, _, out=out, start=start, base=base, sem=sem):
                for m in range(ra):
                    at = pl.multiple_of(((i - start) * ra + m) * bs, bs)
                    source = b.at[cols_s[m, base + i]]
                    pltpu.make_async_copy(source, out.at[pl.ds(at, bs)], sem).start()
                return 0

            lax.fori_loop(start, stop, one_row, 0, unroll=2)
            blocks = out.at[pl.ds(0, (stop - start) * wide)]
            waits.append(pltpu.make_async_copy(blocks, blocks, sem))

    cols = cols_v[...]
    both = [entries(cols, h * half, half, rb) for h in range(2)]
    for flip in range(2):
        named = jnp.where(odd != (flip == 1), both[1], both[0])
        named = jnp.broadcast_to(named, (kw, named.shape[1]))
        picked = lax.broadcasted_iota(I32, named.shape, 0) == named
        picked = jnp.where(picked, 1.0, 0.0).astype(BF16)
        found = jnp.dot(table[...], picked, preferred_element_type=F32)
        slot = lax.broadcasted_iota(I32, (1, found.shape[1]), 1) // (ra * half)
        parts = []
        for part in range(PARTS):
            value = found[part * rb : part * rb + 1]
            for n in range(1, rb):
                value = jnp.where(slot == n, found[part * rb + n : part * rb + n + 1], value)
            parts.append(value)
        tile = stacked(parts, META).astype(BF16)
        for out, (start, stop) in zip(outs[flip], cuts[flip]):
            out[pl.ds((stop - start) * wide, META), :] = tile
    for wait in waits:
        wait.wait()


def gather(parity, cols, table, b, half, cuts, after):
    ra = cols.shape[0]
    bs, width = b.shape[1:]
    rb = width // bs
    smem, vmem = pl.BlockSpec(memory_space=pltpu.SMEM), pl.BlockSpec(memory_space=pltpu.VMEM)
    hbm = pl.BlockSpec(memory_space=pltpu.HBM)
    outs = [
        pltpu.VMEM(((stop - start) * ra * bs + META, width), BF16) for cut in cuts for start, stop in cut
    ]
    got = pl.pallas_call(
        functools.partial(gather_kernel, half, ra, rb, bs, cuts, len(after)),
        out_shape=outs,
        in_specs=[smem, smem, vmem, vmem, hbm] + [pl.BlockSpec(memory_space=pl.ANY)] * len(after),
        out_specs=[vmem] * len(outs),
        scratch_shapes=[pltpu.SemaphoreType.DMA((len(outs),))],
        compiler_params=pltpu.CompilerParams(vmem_limit_bytes=VMEM_LIMIT),
        cost_estimate=pl.CostEstimate(flops=0, bytes_accessed=1024, transcendentals=0),
        name="gather_rows",
    )(parity, cols, cols, in_vmem(table), pltpu.with_memory_space_constraint(b, pltpu.HBM), *after)
    got = list(got)
    return [[got.pop(0) for _ in cut] for cut in cuts]


def add_kernel(ra, rb, bs, flip, rows, flush, has_out, place, *refs):
    refs = list(refs)
    a, b, _ = refs.pop(0), refs.pop(0), refs.pop(0)
    a = a.at[place[0]]
    if has_out:
        refs.pop(0)
    acc, done = refs.pop(0), refs.pop(0)
    done[...] = jnp.zeros(done.shape, done.dtype)
    if flush:
        target = refs.pop(0)
    prod, scl_v, col_v, scl_s, col_s, stage, sems, out_sems = refs
    first, last = rows
    wide = ra * bs
    half, tiles = acc.shape[:2]
    per = LANES // bs
    a_meta = a[flip, pl.ds(a.shape[1] - META, META), :].astype(F32)
    b_meta = b[pl.ds(b.shape[0] - META, META), :].astype(F32)
    scl_a = a_meta[0:1] + a_meta[1:2] + a_meta[2:3]
    scl_b = b_meta[0:1] + b_meta[1:2] + b_meta[2:3]
    scl_v[...] = jnp.broadcast_to(scl_a * scl_b, scl_v.shape)
    col_v[...] = jnp.broadcast_to((b_meta[3:4] * 256.0 + b_meta[4:5]).astype(I32), col_v.shape)
    moves = [
        pltpu.make_async_copy(scl_v, scl_s, sems.at[0]),
        pltpu.make_async_copy(col_v, col_s, sems.at[1]),
    ]
    for move in moves:
        move.start()
    row_block = lax.broadcasted_iota(I32, (wide, wide), 0) // bs
    col_block = lax.broadcasted_iota(I32, (wide, wide), 1) // bs
    diagonal = jnp.where(row_block == col_block, 1.0, 0.0).astype(BF16)
    for i in range(first, last):
        left = a[flip, pl.ds(i * bs, bs), :]
        left = jnp.concatenate([left] * ra, axis=0) * diagonal
        right = b[pl.ds((i - first) * wide, wide), :]
        prod[pl.ds((i - first) * wide, wide), :] = jnp.dot(left, right, preferred_element_type=F32)
    for move in moves:
        move.wait()
    lane_block = lax.broadcasted_iota(I32, (bs, LANES), 1) // bs

    def one_row(i, _):
        for m in range(ra):
            value = prod[pl.ds(pl.multiple_of(((i - first) * ra + m) * bs, bs), bs), :]
            for n in range(rb):
                entry = (n * ra + m) * half + i
                column = col_s[0, entry]
                place = column & (per - 1)
                moved = pltpu.roll(value, ((place - n) & (per - 1)) * bs, 1)
                moved = jnp.where(lane_block == place, moved * scl_s[0, entry], 0.0)
                tile = column // per
                acc[i, tile] = acc[i, tile] + moved
        return 0

    lax.fori_loop(first, last, one_row, 0)
    if flush:

        def send(i):
            slot = (i - first) % 2
            return pltpu.make_async_copy(stage.at[slot], target.at[i], out_sems.at[slot])

        for i in range(first, last):
            if i - first >= 2:
                send(i - 2).wait()
            for tile in range(tiles):
                stage[(i - first) % 2, :, pl.ds(tile * LANES, LANES)] = acc[i, tile].astype(BF16)
            send(i).start()
        for i in range(max(first, last - 2), last):
            send(i).wait()


def add_products(place, a, b, flip, shape, rows, acc, flush=False, out=None):
    half, ra, rb, bs = shape
    out_shapes = [pltpu.VMEM(acc.shape, F32), jax.ShapeDtypeStruct((8, LANES), F32)]
    if flush:
        out_shapes.append(jax.ShapeDtypeStruct((half, bs, JW * bs), BF16))
    vmem = pl.BlockSpec(memory_space=pltpu.VMEM)
    anywhere = pl.BlockSpec(memory_space=pl.ANY)
    args = [place, a, b, in_vmem(acc)]
    specs = [pl.BlockSpec(memory_space=pltpu.SMEM)] + [vmem] * 3
    aliases = {3: 0}
    if out is not None:
        aliases[len(args)] = 2
        args.append(out)
        specs.append(anywhere)
    count = rows[1] - rows[0]
    return pl.pallas_call(
        functools.partial(add_kernel, ra, rb, bs, flip, rows, flush, out is not None),
        out_shape=out_shapes,
        in_specs=specs,
        out_specs=[vmem, vmem, anywhere][: len(out_shapes)],
        input_output_aliases=aliases,
        scratch_shapes=[
            pltpu.VMEM((count * ra * bs, rb * bs), F32),
            pltpu.VMEM((8, LANES), F32),
            pltpu.VMEM((8, LANES), I32),
            pltpu.SMEM((8, LANES), F32),
            pltpu.SMEM((8, LANES), I32),
            pltpu.VMEM((2, bs, JW * bs) if flush else (2, 16, LANES), BF16),
            pltpu.SemaphoreType.DMA((2,)),
            pltpu.SemaphoreType.DMA((2,)),
        ],
        compiler_params=pltpu.CompilerParams(vmem_limit_bytes=VMEM_LIMIT),
        cost_estimate=pl.CostEstimate(flops=0, bytes_accessed=1024, transcendentals=0),
        name="add_products",
    )(*args)


def on_device(a_blocks, a_scale, a_cols, b_blocks, b_scale, b_cols):
    panels = lax.axis_size("row")
    columns = lax.axis_size("col")
    halves = columns // panels
    a_part, a_scl, a_pos = a_blocks[0, 0], a_scale[0, 0].T, a_cols[0, 0].T
    b_part = b_blocks[0, 0]
    b_scl, b_pos = b_scale[0, 0].T, b_cols[0, 0].T
    nrows, bs, _ = a_part.shape
    ra, rb = a_scl.shape[0], b_scl.shape[0]
    half = nrows // halves
    shape = (half, ra, rb, bs)
    parity = (lax.axis_index("col") % halves).astype(I32).reshape(1)

    def step(value, by, flip):
        pairs = [
            (c, ((c // halves + by) % panels) * halves + (c % halves ^ flip)) for c in range(columns)
        ]
        return lax.ppermute(value, "col", pairs)

    def named_by(by):
        pairs = []
        for r in range(panels):
            for c in range(columns):
                to_row = (r + by) % panels
                to_col = (c - halves * by) % columns
                pairs.append((r * columns + c, to_row * columns + to_col))
        return lax.ppermute(a_pos, ("row", "col"), pairs)

    order = sorted(range(1, panels), key=lambda by: -min(by, panels - by))
    asked = {by: named_by(by) for by in order}
    asked[0] = a_pos
    every = (0, half)
    early = (0, half - max(1, half // 4))
    late = (early[1], half)

    table, acc = prepare(b_scl, b_pos, half, bs)

    def messages(by, after):
        cuts = [[every], [early, late] if by == order[-1] else [every]]
        return gather(parity, asked[by], table, b_part, half, cuts, after)

    sent = {}
    after = [asked[by] for by in order[1:]]
    for by in order[:-1] + [0]:
        sent[by] = messages(by, after)
        after = [sent[by][0][0]]
    first = sent[order[0]][0][0]
    kept, given = split(parity, a_part.reshape(nrows * bs, ra * bs), a_scl, half, rb, bs, first)
    left = jnp.stack([kept, step(given, 0, 1)])
    lefts = lax.all_gather(left, "row")
    row = lax.axis_index("row")
    taken = step(sent[0][1][0], 0, 1)
    zero = jnp.zeros((1,), I32)
    acc = add_products(zero, kept[None, None], sent[0][0][0], 0, shape, every, acc)[0]
    acc, done = add_products(zero, left[None], taken, 1, shape, every, acc)
    sent[order[-1]] = messages(order[-1], [done])
    for by in order:
        place = ((row - by) % panels).astype(I32).reshape(1)
        for flip in range(halves):
            arrived = [step(message, by, flip) for message in sent[by][flip]]
            if len(arrived) == 1:
                acc = add_products(place, lefts, arrived[0], flip, shape, every, acc)[0]
            else:
                acc, _, out = add_products(place, lefts, arrived[0], flip, shape, early, acc, flush=True)
                out = add_products(place, lefts, arrived[1], flip, shape, late, acc, flush=True, out=out)[2]
    return out[None, None]


def solution(mesh):
    in_specs = (
        P("col", "row", None, None, None),
        P("col", "row", None, None),
        P("col", "row", None, None),
        P("col", "row", None, None, None),
        P("col", "row", None, None),
        P("col", "row", None, None),
    )
    out_specs = P("col", "row", None, None, None)
    return jax.shard_map(
        on_device, mesh=mesh, in_specs=in_specs, out_specs=out_specs, check_vma=False
    )
```

```python
import functools

import jax
import jax.numpy as jnp
from jax import lax
from jax.experimental import pallas as pl
from jax.experimental.pallas import tpu as pltpu
from jax.sharding import PartitionSpec as P

JW = 512
LANES = 128
META = 16
PARTS = 5
F32, BF16, I32 = jnp.float32, jnp.bfloat16, jnp.int32
VMEM_LIMIT = 12 * 1024 * 1024


def in_vmem(x):
    return pltpu.with_memory_space_constraint(x, pltpu.VMEM)


def three_parts(x):
    high = x.astype(BF16).astype(F32)
    rest = x - high
    mid = rest.astype(BF16).astype(F32)
    return [high, mid, (rest - mid).astype(BF16).astype(F32)]


def stacked(parts, rows):
    which = lax.broadcasted_iota(I32, (rows, parts[0].shape[1]), 0)
    tile = jnp.zeros(which.shape, F32)
    for at, part in enumerate(parts):
        tile = jnp.where(which == at, jnp.broadcast_to(part, which.shape), tile)
    return tile


def entries(values, first, half, rb):
    ra = values.shape[0]
    one = [values[m : m + 1, first : first + half] for m in range(ra)]
    return jnp.concatenate(one * rb, axis=1)


def prepare_kernel(rb, parity, bscale, bcols, table, acc):
    scale, column = bscale[...], bcols[...]
    rows = three_parts(scale) + [(column >> 8).astype(F32), (column & 255).astype(F32)]
    rows.append(jnp.zeros((table.shape[0] - PARTS * rb, table.shape[1]), F32))
    table[...] = jnp.concatenate(rows, axis=0).astype(BF16)
    for i in range(acc.shape[0]):

        def clear(tile, _, i=i):
            acc[i, tile] = jnp.zeros(acc.shape[2:], F32)
            return 0

        lax.fori_loop(0, acc.shape[1], clear, 0, unroll=8)


def prepare(parity, bscale, bcols, half, bs):
    rb, kw = bscale.shape
    vmem = pl.BlockSpec(memory_space=pltpu.VMEM)
    return pl.pallas_call(
        functools.partial(prepare_kernel, rb),
        out_shape=[
            pltpu.VMEM((-(-PARTS * rb // 16) * 16, kw), BF16),
            pltpu.VMEM((half, JW * bs // LANES, bs, LANES), F32),
        ],
        in_specs=[pl.BlockSpec(memory_space=pltpu.SMEM)] + [vmem] * 2,
        out_specs=[vmem] * 2,
        compiler_params=pltpu.CompilerParams(vmem_limit_bytes=VMEM_LIMIT),
        cost_estimate=pl.CostEstimate(flops=2 * 10**10, bytes_accessed=2**20, transcendentals=0),
        name="prepare",
    )(parity, bscale, bcols)


def split_kernel(half, rb, bs, parity, a, ascale, after, kept, given):
    scale = ascale[...]
    both = [entries(scale, h * half, half, rb) for h in range(2)]
    odd = parity[0] == 1
    for flip, out in enumerate((kept, given)):
        base = (parity[0] ^ flip) * half
        out[pl.ds(0, half * bs), :] = a[pl.ds(pl.multiple_of(base * bs, bs), half * bs), :]
        parts = three_parts(jnp.where(odd != (flip == 1), both[1], both[0]))
        out[pl.ds(half * bs, META), :] = stacked(parts, META).astype(BF16)


def split(parity, a, ascale, half, rb, bs, after):
    smem, vmem = pl.BlockSpec(memory_space=pltpu.SMEM), pl.BlockSpec(memory_space=pltpu.VMEM)
    return pl.pallas_call(
        functools.partial(split_kernel, half, rb, bs),
        out_shape=[pltpu.VMEM((half * bs + META, a.shape[1]), BF16)] * 2,
        in_specs=[smem, vmem, vmem, pl.BlockSpec(memory_space=pl.ANY)],
        out_specs=[vmem] * 2,
        compiler_params=pltpu.CompilerParams(vmem_limit_bytes=VMEM_LIMIT),
        cost_estimate=pl.CostEstimate(flops=2 * 10**10, bytes_accessed=2**20, transcendentals=0),
        name="split",
    )(parity, a, ascale, after)


def join_kernel(own, taken, both):
    count = own.shape[0]
    both[pl.ds(0, count)] = own[...]
    both[pl.ds(count, count)] = taken[...]


def join(own, taken):
    vmem = pl.BlockSpec(memory_space=pltpu.VMEM)
    return pl.pallas_call(
        join_kernel,
        out_shape=pltpu.VMEM((2 * own.shape[0],) + own.shape[1:], BF16),
        in_specs=[vmem] * 2,
        out_specs=vmem,
        compiler_params=pltpu.CompilerParams(vmem_limit_bytes=VMEM_LIMIT),
        cost_estimate=pl.CostEstimate(flops=2 * 10**10, bytes_accessed=2**20, transcendentals=0),
        name="join",
    )(in_vmem(own), taken)


def gather_kernel(half, ra, rb, bs, cuts, afters, parity, cols_s, cols_v, table, b, *refs):
    refs = list(refs)[afters:]
    outs = [[refs.pop(0) for _ in cut] for cut in cuts]
    (sems,) = refs
    wide = ra * bs
    kw = b.shape[0]
    odd = parity[0] == 1

    waits = []
    for flip in range(2):
        base = (parity[0] ^ flip) * half
        for out, (start, stop) in zip(outs[flip], cuts[flip]):
            sem = sems.at[len(waits)]

            def one_row(i, _, out=out, start=start, base=base, sem=sem):
                for m in range(ra):
                    at = pl.multiple_of(((i - start) * ra + m) * bs, bs)
                    source = b.at[cols_s[m, base + i]]
                    pltpu.make_async_copy(source, out.at[pl.ds(at, bs)], sem).start()
                return 0

            lax.fori_loop(start, stop, one_row, 0, unroll=2)
            blocks = out.at[pl.ds(0, (stop - start) * wide)]
            waits.append(pltpu.make_async_copy(blocks, blocks, sem))

    cols = cols_v[...]
    both = [entries(cols, h * half, half, rb) for h in range(2)]
    for flip in [flip for flip in range(2) if cuts[flip]]:
        named = jnp.where(odd != (flip == 1), both[1], both[0])
        named = jnp.broadcast_to(named, (kw, named.shape[1]))
        picked = lax.broadcasted_iota(I32, named.shape, 0) == named
        picked = jnp.where(picked, 1.0, 0.0).astype(BF16)
        found = jnp.dot(table[...], picked, preferred_element_type=F32)
        slot = lax.broadcasted_iota(I32, (1, found.shape[1]), 1) // (ra * half)
        parts = []
        for part in range(PARTS):
            value = found[part * rb : part * rb + 1]
            for n in range(1, rb):
                value = jnp.where(slot == n, found[part * rb + n : part * rb + n + 1], value)
            parts.append(value)
        tile = stacked(parts, META).astype(BF16)
        for out, (start, stop) in zip(outs[flip], cuts[flip]):
            out[pl.ds((stop - start) * wide, META), :] = tile
    for wait in waits:
        wait.wait()


def gather(parity, cols, table, b, half, cuts, after):
    ra = cols.shape[0]
    bs, width = b.shape[1:]
    rb = width // bs
    smem, vmem = pl.BlockSpec(memory_space=pltpu.SMEM), pl.BlockSpec(memory_space=pltpu.VMEM)
    hbm = pl.BlockSpec(memory_space=pltpu.HBM)
    outs = [
        pltpu.VMEM(((stop - start) * ra * bs + META, width), BF16) for cut in cuts for start, stop in cut
    ]
    got = pl.pallas_call(
        functools.partial(gather_kernel, half, ra, rb, bs, cuts, len(after)),
        out_shape=outs,
        in_specs=[smem, smem, vmem, vmem, hbm] + [pl.BlockSpec(memory_space=pl.ANY)] * len(after),
        out_specs=[vmem] * len(outs),
        scratch_shapes=[pltpu.SemaphoreType.DMA((len(outs),))],
        compiler_params=pltpu.CompilerParams(vmem_limit_bytes=VMEM_LIMIT),
        cost_estimate=pl.CostEstimate(flops=2 * 10**10, bytes_accessed=2**20, transcendentals=0),
        name="gather_rows",
    )(parity, cols, cols, in_vmem(table), pltpu.with_memory_space_constraint(b, pltpu.HBM), *after)
    got = list(got)
    return [[got.pop(0) for _ in cut] for cut in cuts]


def add_kernel(ra, rb, bs, by, flip, rows, flush, afters, has_out, info, *refs):
    refs = list(refs)
    a, b, _ = refs.pop(0), refs.pop(0), refs.pop(0)
    refs = refs[afters:]
    a = a.at[info[1 + by]]
    if has_out:
        refs.pop(0)
    acc, done = refs.pop(0), refs.pop(0)
    done[...] = jnp.zeros(done.shape, done.dtype)
    if flush:
        target = refs.pop(0)
    prod, scl_v, col_v, scl_s, col_s, stage, sems, out_sems = refs
    first, last = rows
    wide = ra * bs
    half, tiles = acc.shape[:2]
    per = LANES // bs
    a_meta = a[flip, pl.ds(a.shape[1] - META, META), :].astype(F32)
    b_meta = b[pl.ds(b.shape[0] - META, META), :].astype(F32)
    scl_a = a_meta[0:1] + a_meta[1:2] + a_meta[2:3]
    scl_b = b_meta[0:1] + b_meta[1:2] + b_meta[2:3]
    scl_v[...] = jnp.broadcast_to(scl_a * scl_b, scl_v.shape)
    col_v[...] = jnp.broadcast_to((b_meta[3:4] * 256.0 + b_meta[4:5]).astype(I32), col_v.shape)
    moves = [
        pltpu.make_async_copy(scl_v, scl_s, sems.at[0]),
        pltpu.make_async_copy(col_v, col_s, sems.at[1]),
    ]
    for move in moves:
        move.start()
    row_block = lax.broadcasted_iota(I32, (wide, wide), 0) // bs
    col_block = lax.broadcasted_iota(I32, (wide, wide), 1) // bs
    diagonal = jnp.where(row_block == col_block, 1.0, 0.0).astype(BF16)
    for i in range(first, last):
        left = a[flip, pl.ds(i * bs, bs), :]
        left = jnp.concatenate([left] * ra, axis=0) * diagonal
        right = b[pl.ds((i - first) * wide, wide), :]
        prod[pl.ds((i - first) * wide, wide), :] = jnp.dot(left, right, preferred_element_type=F32)
    for move in moves:
        move.wait()
    lane_block = lax.broadcasted_iota(I32, (bs, LANES), 1) // bs

    def one_row(i, _):
        for m in range(ra):
            value = prod[pl.ds(pl.multiple_of(((i - first) * ra + m) * bs, bs), bs), :]
            for n in range(rb):
                entry = (n * ra + m) * half + i
                column = col_s[0, entry]
                place = column & (per - 1)
                moved = pltpu.roll(value, ((place - n) & (per - 1)) * bs, 1)
                moved = jnp.where(lane_block == place, moved * scl_s[0, entry], 0.0)
                tile = column // per
                acc[i, tile] = acc[i, tile] + moved
        return 0

    lax.fori_loop(first, last, one_row, 0)
    if flush:

        def send(i):
            slot = (i - first) % 2
            return pltpu.make_async_copy(stage.at[slot], target.at[i], out_sems.at[slot])

        for i in range(first, last):
            if i - first >= 2:
                send(i - 2).wait()
            for tile in range(tiles):
                stage[(i - first) % 2, :, pl.ds(tile * LANES, LANES)] = acc[i, tile].astype(BF16)
            send(i).start()
        for i in range(max(first, last - 2), last):
            send(i).wait()


def add_products(info, a, b, by, flip, shape, rows, acc, flush=False, out=None, after=()):
    half, ra, rb, bs = shape
    out_shapes = [pltpu.VMEM(acc.shape, F32), jax.ShapeDtypeStruct((8, LANES), F32)]
    if flush:
        out_shapes.append(jax.ShapeDtypeStruct((half, bs, JW * bs), BF16))
    vmem = pl.BlockSpec(memory_space=pltpu.VMEM)
    anywhere = pl.BlockSpec(memory_space=pl.ANY)
    args = [info, in_vmem(a), b, in_vmem(acc)]
    specs = [pl.BlockSpec(memory_space=pltpu.SMEM)] + [vmem] * 3
    aliases = {3: 0}
    args += after
    specs += [anywhere] * len(after)
    if out is not None:
        aliases[len(args)] = 2
        args.append(out)
        specs.append(anywhere)
    count = rows[1] - rows[0]
    return pl.pallas_call(
        functools.partial(add_kernel, ra, rb, bs, by, flip, rows, flush, len(after), out is not None),
        out_shape=out_shapes,
        in_specs=specs,
        out_specs=[vmem, vmem, anywhere][: len(out_shapes)],
        input_output_aliases=aliases,
        scratch_shapes=[
            pltpu.VMEM((count * ra * bs, rb * bs), F32),
            pltpu.VMEM((8, LANES), F32),
            pltpu.VMEM((8, LANES), I32),
            pltpu.SMEM((8, LANES), F32),
            pltpu.SMEM((8, LANES), I32),
            pltpu.VMEM((2, bs, JW * bs) if flush else (2, 16, LANES), BF16),
            pltpu.SemaphoreType.DMA((2,)),
            pltpu.SemaphoreType.DMA((2,)),
        ],
        compiler_params=pltpu.CompilerParams(vmem_limit_bytes=VMEM_LIMIT),
        cost_estimate=pl.CostEstimate(flops=2 * 10**10, bytes_accessed=2**20, transcendentals=0),
        name="add_products",
    )(*args)


def on_device(a_blocks, a_scale, a_cols, b_blocks, b_scale, b_cols):
    panels = lax.axis_size("row")
    columns = lax.axis_size("col")
    halves = columns // panels
    a_part, a_scl, a_pos = a_blocks[0, 0], a_scale[0, 0].T, a_cols[0, 0].T
    b_part = b_blocks[0, 0]
    b_scl, b_pos = b_scale[0, 0].T, b_cols[0, 0].T
    nrows, bs, _ = a_part.shape
    ra, rb = a_scl.shape[0], b_scl.shape[0]
    half = nrows // halves
    shape = (half, ra, rb, bs)
    row = lax.axis_index("row")
    parity = lax.axis_index("col") % halves
    info = jnp.stack([parity] + [row ^ ((row - by) % panels) for by in range(panels)]).astype(I32)

    def step(value, by, flip):
        pairs = [
            (c, ((c // halves + by) % panels) * halves + (c % halves ^ flip)) for c in range(columns)
        ]
        return lax.ppermute(value, "col", pairs)

    def named_by(by):
        pairs = []
        for r in range(panels):
            for c in range(columns):
                to_row = (r + by) % panels
                to_col = (c - halves * by) % columns
                pairs.append((r * columns + c, to_row * columns + to_col))
        return lax.ppermute(a_pos, ("row", "col"), pairs)

    order = sorted(range(1, panels), key=lambda by: -min(by, panels - by))
    asked = {by: named_by(by) for by in order}
    asked[0] = a_pos
    every = (0, half)
    early = (0, half - max(1, half // 4))
    late = (early[1], half)

    table, acc = prepare(info, b_scl, b_pos, half, bs)

    def messages(by, cuts, after):
        return gather(info, asked[by], table, b_part, half, cuts, after)

    whole = [[every], [every]]
    sent = {order[0]: messages(order[0], whole, [asked[by] for by in order[1:]])}
    first = sent[order[0]][0][0]
    kept, given = split(info, a_part.reshape(nrows * bs, ra * bs), a_scl, half, rb, bs, first)
    left = join(kept[None], step(given, 0, 1)[None])[None]
    own_left = left
    bit = 1
    while bit < panels:
        left = join(left, lax.ppermute(left, "row", [(r, r ^ bit) for r in range(panels)]))
        bit *= 2
    after = [first]
    for by in order[1:-1] + [0]:
        sent[by] = messages(by, whole, after)
        after = [sent[by][0][0]]
    taken = step(sent[0][1][0], 0, 1)
    acc, done = add_products(info, own_left, sent[0][0][0], 0, 0, shape, every, acc)
    last = order[-1]
    ends = [messages(last, [[every], []], [done, left])[0][0]]
    for by in order[:-1]:
        for flip in range(halves):
            arrived = step(sent[by][flip][0], by, flip)
            after = ends[-1:] if by == order[0] else []
            acc, done = add_products(info, left, arrived, by, flip, shape, every, acc, after=after)
            if by == order[0]:
                rows = early if flip == 0 else late
                ends.append(messages(last, [[], [rows]], [done])[1][0])
        if by == order[0]:
            acc = add_products(info, left, taken, 0, 1, shape, every, acc)[0]
    arrived = step(ends[0], last, 0)
    acc = add_products(info, left, arrived, last, 0, shape, every, acc)[0]
    arrived = step(ends[1], last, 1)
    acc, _, out = add_products(info, left, arrived, last, 1, shape, early, acc, flush=True)
    arrived = step(ends[2], last, 1)
    out = add_products(info, left, arrived, last, 1, shape, late, acc, flush=True, out=out)[2]
    return out[None, None]


def solution(mesh):
    in_specs = (
        P("col", "row", None, None, None),
        P("col", "row", None, None),
        P("col", "row", None, None),
        P("col", "row", None, None, None),
        P("col", "row", None, None),
        P("col", "row", None, None),
    )
    out_specs = P("col", "row", None, None, None)
    return jax.shard_map(
        on_device, mesh=mesh, in_specs=in_specs, out_specs=out_specs, check_vma=False
    )
```

```python
import functools

import jax
import jax.numpy as jnp
from jax import lax
from jax.experimental import pallas as pl
from jax.experimental.pallas import tpu as pltpu
from jax.sharding import PartitionSpec as P

JW = 512
LANES = 128
META = 16
PARTS = 5
CHUNKS = 4
F32, BF16, I32 = jnp.float32, jnp.bfloat16, jnp.int32
VMEM_LIMIT = 12 * 1024 * 1024


def three_parts(x):
    high = x.astype(BF16).astype(F32)
    rest = x - high
    mid = rest.astype(BF16).astype(F32)
    return [high, mid, (rest - mid).astype(BF16).astype(F32)]


def stacked(parts, rows):
    which = lax.broadcasted_iota(I32, (rows, parts[0].shape[1]), 0)
    tile = jnp.zeros(which.shape, F32)
    for at, part in enumerate(parts):
        tile = jnp.where(which == at, jnp.broadcast_to(part, which.shape), tile)
    return tile


def entries(values, first, half, rb):
    ra = values.shape[0]
    one = [values[m : m + 1, first : first + half] for m in range(ra)]
    return jnp.concatenate(one * rb, axis=1)


class Sizes:
    def __init__(self, half, ra, rb, bs):
        self.half, self.ra, self.rb, self.bs = half, ra, rb, bs
        self.wide = ra * bs
        self.tiles = JW * bs // LANES

    def message(self, rows):
        return pltpu.VMEM(((rows[1] - rows[0]) * self.wide + META, self.rb * self.bs), BF16)

    def window(self):
        return pltpu.VMEM((self.half, self.tiles, self.bs, LANES), F32)


def kernel_call(name, body, ins, outs, aliases=(), scratch=None):
    scratch = scratch or {}
    names = list(ins) + list(outs) + list(scratch)

    def kernel(*refs):
        body(dict(zip(names, refs)))

    args, in_specs = [], []
    for array, place in ins.values():
        if place == "smem":
            spec = pl.BlockSpec(memory_space=pltpu.SMEM)
        elif place == "vmem":
            spec = pl.BlockSpec(memory_space=pltpu.VMEM)
            array = pltpu.with_memory_space_constraint(array, pltpu.VMEM)
        elif place == "hbm":
            spec = pl.BlockSpec(memory_space=pltpu.HBM)
            array = pltpu.with_memory_space_constraint(array, pltpu.HBM)
        else:
            spec = pl.BlockSpec(memory_space=pl.ANY)
        args.append(array)
        in_specs.append(spec)
    out_specs = [
        pl.BlockSpec(memory_space=pl.ANY if isinstance(shape, jax.ShapeDtypeStruct) else pltpu.VMEM)
        for shape in outs.values()
    ]
    got = pl.pallas_call(
        kernel,
        out_shape=list(outs.values()),
        in_specs=in_specs,
        out_specs=out_specs,
        input_output_aliases={list(ins).index(a): list(outs).index(b) for a, b in aliases},
        scratch_shapes=list(scratch.values()),
        compiler_params=pltpu.CompilerParams(vmem_limit_bytes=VMEM_LIMIT),
        cost_estimate=pl.CostEstimate(flops=FLOPS, bytes_accessed=1024, transcendentals=0),
        name=name,
    )(*args)
    return dict(zip(outs, got))


FLOPS = 0


class Gather:
    def __init__(self, sizes, refs, out, flip, rows, cols, sem):
        self.z, self.refs, self.out, self.flip, self.rows, self.cols = sizes, refs, refs[out], flip, rows, cols
        self.sem = sem

    def start(self):
        z, refs = self.z, self.refs
        cols, b = refs[self.cols + "_s"], refs["b"]
        base = (refs["info"][0] ^ self.flip) * z.half
        first, last = self.rows

        def one_row(i, _):
            for m in range(z.ra):
                at = pl.multiple_of(((i - first) * z.ra + m) * z.bs, z.bs)
                source = b.at[cols[m, base + i]]
                pltpu.make_async_copy(source, self.out.at[pl.ds(at, z.bs)], self.sem).start()
            return 0

        lax.fori_loop(first, last, one_row, 0, unroll=2)

    def finish(self):
        z, refs = self.z, self.refs
        table, cols = refs["table"], refs[self.cols + "_v"][...]
        kw = table.shape[1]
        both = [entries(cols, h * z.half, z.half, z.rb) for h in range(2)]
        odd = (refs["info"][0] ^ self.flip) == 1
        named = jnp.where(odd, both[1], both[0])
        named = jnp.broadcast_to(named, (kw, named.shape[1]))
        picked = lax.broadcasted_iota(I32, named.shape, 0) == named
        picked = jnp.where(picked, 1.0, 0.0).astype(BF16)
        found = jnp.dot(table[...], picked, preferred_element_type=F32)
        slot = lax.broadcasted_iota(I32, (1, found.shape[1]), 1) // (z.ra * z.half)
        parts = []
        for part in range(PARTS):
            value = found[part * z.rb : part * z.rb + 1]
            for n in range(1, z.rb):
                value = jnp.where(slot == n, found[part * z.rb + n : part * z.rb + n + 1], value)
            parts.append(value)
        size = (self.rows[1] - self.rows[0]) * z.wide
        self.out[pl.ds(size, META), :] = stacked(parts, META).astype(BF16)
        blocks = self.out.at[pl.ds(0, size)]
        pltpu.make_async_copy(blocks, blocks, self.sem).wait()


class Add:
    def __init__(self, sizes, refs, a, b, rows):
        self.z, self.refs, self.a, self.b, self.rows = sizes, refs, a, b, rows

    @staticmethod
    def scratch(sizes, rows):
        return {
            "prod": pltpu.VMEM(((rows[1] - rows[0]) * sizes.wide, LANES), F32),
            "scl_v": pltpu.VMEM((8, LANES), F32),
            "col_v": pltpu.VMEM((8, LANES), I32),
            "scl_s": pltpu.SMEM((8, LANES), F32),
            "col_s": pltpu.SMEM((8, LANES), I32),
            "add_sems": pltpu.SemaphoreType.DMA((2,)),
        }

    def start(self):
        z, refs, a, b = self.z, self.refs, self.a, self.b
        first, last = self.rows
        scl_v, col_v = refs["scl_v"], refs["col_v"]
        a_meta = a[pl.ds(a.shape[0] - META, META), :].astype(F32)
        b_meta = b[pl.ds(b.shape[0] - META, META), :].astype(F32)
        scl_a = a_meta[0:1] + a_meta[1:2] + a_meta[2:3]
        scl_b = b_meta[0:1] + b_meta[1:2] + b_meta[2:3]
        scl_v[...] = jnp.broadcast_to(scl_a * scl_b, scl_v.shape)
        col_v[...] = jnp.broadcast_to((b_meta[3:4] * 256.0 + b_meta[4:5]).astype(I32), col_v.shape)
        sems = refs["add_sems"]
        self.moves = [
            pltpu.make_async_copy(scl_v, refs["scl_s"], sems.at[0]),
            pltpu.make_async_copy(col_v, refs["col_s"], sems.at[1]),
        ]
        for move in self.moves:
            move.start()
        row_block = lax.broadcasted_iota(I32, (z.wide, z.wide), 0) // z.bs
        col_block = lax.broadcasted_iota(I32, (z.wide, z.wide), 1) // z.bs
        diagonal = jnp.where(row_block == col_block, 1.0, 0.0).astype(BF16)
        for i in range(first, last):
            left = a[pl.ds(i * z.bs, z.bs), :]
            left = jnp.concatenate([left] * z.ra, axis=0) * diagonal
            rows = pl.ds((i - first) * z.wide, z.wide)
            refs["prod"][rows, :] = jnp.dot(left, b[rows, :], preferred_element_type=F32)

    def finish(self):
        z, refs = self.z, self.refs
        first, last = self.rows
        acc, prod, scl_s, col_s = refs["acc"], refs["prod"], refs["scl_s"], refs["col_s"]
        per = LANES // z.bs
        for move in self.moves:
            move.wait()
        lane_block = lax.broadcasted_iota(I32, (z.bs, LANES), 1) // z.bs

        def one_row(i, _):
            for m in range(z.ra):
                value = prod[pl.ds(pl.multiple_of(((i - first) * z.ra + m) * z.bs, z.bs), z.bs), :]
                placed = []
                for n in range(z.rb):
                    entry = (n * z.ra + m) * z.half + i
                    column = col_s[0, entry]
                    place = column & (per - 1)
                    moved = pltpu.roll(value, ((place - n) & (per - 1)) * z.bs, 1)
                    moved = jnp.where(lane_block == place, moved * scl_s[0, entry], 0.0)
                    placed.append((column // per, moved))
                for tile, moved in placed:
                    acc[i, tile] = acc[i, tile] + moved
            return 0

        lax.fori_loop(first, last, one_row, 0)


def clear(acc):
    for i in range(acc.shape[0]):

        def clear_tile(tile, _, i=i):
            acc[i, tile] = jnp.zeros(acc.shape[2:], F32)
            return 0

        lax.fori_loop(0, acc.shape[1], clear_tile, 0, unroll=8)


def write_out(sizes, refs, rows):
    acc, stage, sems, out = refs["acc"], refs["stage"], refs["out_sems"], refs["out"]
    slots = stage.shape[0]
    tiles = sizes.tiles // CHUNKS
    pieces = [(i, chunk) for i in range(*rows) for chunk in range(CHUNKS)]

    def send(at):
        i, chunk = pieces[at]
        columns = pl.ds(chunk * tiles * LANES, tiles * LANES)
        return pltpu.make_async_copy(stage.at[at % slots], out.at[i, :, columns], sems.at[at % slots])

    for at, (i, chunk) in enumerate(pieces):
        if at >= slots:
            send(at - slots).wait()
        for tile in range(tiles):
            stage[at % slots, :, pl.ds(tile * LANES, LANES)] = acc[i, chunk * tiles + tile].astype(BF16)
        send(at).start()
    for at in range(max(0, len(pieces) - slots), len(pieces)):
        send(at).wait()


def first_answer(z, info, cols, own_cols, b_scl, b_pos, b, rows):
    rb, kw = b_scl.shape

    def body(refs):
        answer = Gather(z, refs, "message", 0, rows, "cols", refs["sems"].at[0])
        moves = [
            pltpu.make_async_copy(refs["b_scl"], refs["scl"], refs["sems"].at[1]),
            pltpu.make_async_copy(refs["b_pos"], refs["pos"], refs["sems"].at[2]),
        ]
        for move in moves:
            move.start()
        answer.start()
        refs["own"][...] = refs["own_cols"][...]
        for move in moves:
            move.wait()
        scale, column = refs["scl"][...], refs["pos"][...]
        table = three_parts(scale) + [(column >> 8).astype(F32), (column & 255).astype(F32)]
        table.append(jnp.zeros((refs["table"].shape[0] - PARTS * rb, kw), F32))
        refs["table"][...] = jnp.concatenate(table, axis=0).astype(BF16)
        answer.finish()

    return kernel_call(
        "first_answer",
        body,
        {
            "info": (info, "smem"),
            "cols_s": (cols, "smem"),
            "cols_v": (cols, "vmem"),
            "own_cols": (own_cols, "vmem"),
            "b_scl": (b_scl, "hbm"),
            "b_pos": (b_pos, "hbm"),
            "b": (b, "hbm"),
        },
        {
            "table": pltpu.VMEM((-(-PARTS * rb // 16) * 16, kw), BF16),
            "message": z.message(rows),
            "own": pltpu.VMEM(own_cols.shape, I32),
        },
        scratch={
            "scl": pltpu.VMEM(b_scl.shape, F32),
            "pos": pltpu.VMEM(b_pos.shape, I32),
            "sems": pltpu.SemaphoreType.DMA((3,)),
        },
    )


def second_answer(z, info, cols, table, b, rows, a, a_scl, panels):
    def body(refs):
        answer = Gather(z, refs, "message", 1, rows, "cols", refs["sems"].at[0])
        answer.start()
        scale = refs["a_scl"][...]
        size = z.half * z.bs
        spread = refs["spread"]
        for side in range(2):
            blocks = refs["a"][pl.ds(side * size, size), :]
            scales = stacked(three_parts(entries(scale, side * z.half, z.half, z.rb)), META).astype(BF16)
            for panel in range(panels):
                spread[2 * panel + side, pl.ds(0, size), :] = blocks
                spread[2 * panel + side, pl.ds(size, META), :] = scales
        answer.finish()

    return kernel_call(
        "second_answer",
        body,
        {
            "info": (info, "smem"),
            "cols_s": (cols, "smem"),
            "cols_v": (cols, "vmem"),
            "table": (table, "vmem"),
            "b": (b, "hbm"),
            "a": (a, "vmem"),
            "a_scl": (a_scl, "vmem"),
        },
        {
            "message": z.message(rows),
            "spread": pltpu.VMEM((2 * panels, z.half * z.bs + META, z.wide), BF16),
        },
        scratch={"sems": pltpu.SemaphoreType.DMA((1,))},
    )


def own_blocks(z, info, cols, table, b, rows, left, acc):
    def body(refs):
        answer = Gather(z, refs, "message", 1, rows, "cols", refs["sems"].at[0])
        local = Gather(z, refs, "local", 0, rows, "cols", refs["sems"].at[1])
        local.start()
        answer.start()
        local.finish()
        add = Add(z, refs, refs["left"].at[refs["info"][1]], refs["local"], rows)
        add.start()
        answer.finish()
        add.finish()

    return kernel_call(
        "own_blocks",
        body,
        {
            "info": (info, "smem"),
            "cols_s": (cols, "smem"),
            "cols_v": (cols, "vmem"),
            "table": (table, "vmem"),
            "b": (b, "hbm"),
            "left": (left, "vmem"),
            "acc_in": (acc, "vmem"),
        },
        {"acc": z.window(), "message": z.message(rows)},
        aliases=[("acc_in", "acc")],
        scratch={
            "sems": pltpu.SemaphoreType.DMA((2,)),
            "local": z.message(rows),
            **Add.scratch(z, rows),
        },
    )


def add_message(z, info, left, by, flip, message, rows, acc, answers=(), table=None, b=None, write=False, out=None):
    ins = {
        "info": (info, "smem"),
        "left": (left, "vmem"),
        "arrived": (message, "vmem"),
    }
    outs = {"acc": z.window()}
    aliases = []
    if acc is not None:
        ins["acc_in"] = (acc, "vmem")
        aliases.append(("acc_in", "acc"))
    scratch = Add.scratch(z, rows)
    if answers:
        ins.update(table=(table, "vmem"), b=(b, "hbm"))
        scratch["sems"] = pltpu.SemaphoreType.DMA((len(answers),))
    for at, (cols, _, span) in enumerate(answers):
        ins[f"cols{at}_s"] = (cols, "smem")
        ins[f"cols{at}_v"] = (cols, "vmem")
        outs[f"message{at}"] = z.message(span)
    if write:
        outs["out"] = jax.ShapeDtypeStruct((z.half, z.bs, JW * z.bs), BF16)
        scratch["stage"] = pltpu.VMEM((8, z.bs, JW * z.bs // CHUNKS), BF16)
        scratch["out_sems"] = pltpu.SemaphoreType.DMA((8,))
        if out is not None:
            ins["out_in"] = (out, "any")
            aliases.append(("out_in", "out"))

    def body(refs):
        gathers = [
            Gather(z, refs, f"message{at}", side, span, f"cols{at}", refs["sems"].at[at])
            for at, (_, side, span) in enumerate(answers)
        ]
        for gather in gathers:
            gather.start()
        place = refs["info"][1 + 2 * by + flip]
        add = Add(z, refs, refs["left"].at[place], refs["arrived"], rows)
        add.start()
        if acc is None:
            clear(refs["acc"])
        for gather in gathers:
            gather.finish()
        add.finish()
        if write:
            write_out(z, refs, rows)

    got = kernel_call("add_message", body, ins, outs, aliases, scratch)
    return got["acc"], [got[f"message{at}"] for at in range(len(answers))], got.get("out")


def on_device(a_blocks, a_scale, a_cols, b_blocks, b_scale, b_cols):
    panels = lax.axis_size("row")
    columns = lax.axis_size("col")
    halves = columns // panels
    a_part, a_scl, a_pos = a_blocks[0, 0], a_scale[0, 0].T, a_cols[0, 0].T
    b_part = b_blocks[0, 0]
    b_scl, b_pos = b_scale[0, 0].T, b_cols[0, 0].T
    nrows, bs, _ = a_part.shape
    half = nrows // halves
    z = Sizes(half, a_scl.shape[0], b_scl.shape[0], bs)
    row = lax.axis_index("row")
    parity = lax.axis_index("col") % halves
    places = [(row - by) % panels * halves + (parity ^ flip) for by in range(panels) for flip in range(halves)]
    info = jnp.stack([parity] + places).astype(I32)

    def step(value, by, flip):
        pairs = [
            (c, ((c // halves + by) % panels) * halves + (c % halves ^ flip)) for c in range(columns)
        ]
        return lax.ppermute(value, "col", pairs)

    def named_by(by, cols):
        pairs = []
        for r in range(panels):
            for c in range(columns):
                to_row = (r + by) % panels
                to_col = (c - halves * by) % columns
                pairs.append((r * columns + c, to_row * columns + to_col))
        return lax.ppermute(cols, ("row", "col"), pairs)

    order = sorted(range(1, panels), key=lambda by: -min(by, panels - by))
    every = (0, half)
    early = (0, half - max(1, half // 4))
    late = (early[1], half)
    queue = [(by, flip, every) for by in order for flip in range(halves)]
    queue[-1:] = [(order[-1], 1, early), (order[-1], 1, late)]

    asked = {order[0]: named_by(order[0], a_pos)}
    got = first_answer(z, info, asked[order[0]], a_pos, b_scl, b_pos, b_part, every)
    table, own_cols = got["table"], got["own"]
    moving = [step(got["message"], order[0], 0)]
    for by in order[1:]:
        asked[by] = named_by(by, own_cols)
    a_flat = a_part.reshape(nrows * bs, z.wide)
    got = second_answer(z, info, asked[order[0]], table, b_part, every, a_flat, a_scl, panels)
    moving.append(step(got["message"], order[0], 1))

    groups = [
        [r * columns + c for r in range(panels) for c in range(s * halves, (s + 1) * halves)]
        for s in range(panels)
    ]
    left = lax.all_to_all(got["spread"], ("row", "col"), 0, 0, axis_index_groups=groups)

    acc = None
    taken = None
    out = None
    for at, (by, flip, rows) in enumerate(queue):
        upto = min(len(queue), at + (3 if at == 0 else 4))
        if upto == len(queue) - 1:
            upto = len(queue)
        later = queue[len(moving) : upto]
        if at == len(queue) - 2:
            acc = add_message(z, info, left, 0, 1, taken, every, acc)[0]
        write = at >= len(queue) - 2
        acc, answers, out = add_message(
            z, info, left, by, flip, moving[at], rows, acc,
            answers=[(asked[to], side, span) for to, side, span in later],
            table=table, b=b_part, write=write, out=out,
        )
        for answer, (to, side, _) in zip(answers, later):
            moving.append(step(answer, to, side))
        if at == 0:
            mine = own_blocks(z, info, own_cols, table, b_part, every, left, acc)
            acc = mine["acc"]
            taken = step(mine["message"], 0, 1)
    return out[None, None]


def solution(mesh):
    in_specs = (
        P("col", "row", None, None, None),
        P("col", "row", None, None),
        P("col", "row", None, None),
        P("col", "row", None, None, None),
        P("col", "row", None, None),
        P("col", "row", None, None),
    )
    out_specs = P("col", "row", None, None, None)
    return jax.shard_map(
        on_device, mesh=mesh, in_specs=in_specs, out_specs=out_specs, check_vma=False
    )
```

```python
import functools

import jax
import jax.numpy as jnp
from jax import lax
from jax.experimental import pallas as pl
from jax.experimental.pallas import tpu as pltpu
from jax.sharding import PartitionSpec as P

JW = 512
LANES = 128
META = 16
PARTS = 5
CHUNKS = 4
F32, BF16, I32 = jnp.float32, jnp.bfloat16, jnp.int32
VMEM_LIMIT = 12 * 1024 * 1024


def three_parts(x):
    high = x.astype(BF16).astype(F32)
    rest = x - high
    mid = rest.astype(BF16).astype(F32)
    return [high, mid, (rest - mid).astype(BF16).astype(F32)]


def stacked(parts, rows):
    which = lax.broadcasted_iota(I32, (rows, parts[0].shape[1]), 0)
    tile = jnp.zeros(which.shape, F32)
    for at, part in enumerate(parts):
        tile = jnp.where(which == at, jnp.broadcast_to(part, which.shape), tile)
    return tile


def entries(values, first, half, rb):
    ra = values.shape[0]
    one = [values[m : m + 1, first : first + half] for m in range(ra)]
    return jnp.concatenate(one * rb, axis=1)


class Sizes:
    def __init__(self, half, ra, rb, bs):
        self.half, self.ra, self.rb, self.bs = half, ra, rb, bs
        self.wide = ra * bs
        self.tiles = JW * bs // LANES

    def message(self, rows):
        return pltpu.VMEM(((rows[1] - rows[0]) * self.wide + META, self.rb * self.bs), BF16)

    def window(self):
        return pltpu.VMEM((self.half, self.tiles, self.bs, LANES), F32)


def kernel_call(name, body, ins, outs, aliases=(), scratch=None):
    scratch = scratch or {}
    names = list(ins) + list(outs) + list(scratch)

    def kernel(*refs):
        body(dict(zip(names, refs)))

    args, in_specs = [], []
    for array, place in ins.values():
        if place == "smem":
            spec = pl.BlockSpec(memory_space=pltpu.SMEM)
        elif place == "vmem":
            spec = pl.BlockSpec(memory_space=pltpu.VMEM)
            array = pltpu.with_memory_space_constraint(array, pltpu.VMEM)
        elif place == "hbm":
            spec = pl.BlockSpec(memory_space=pltpu.HBM)
            array = pltpu.with_memory_space_constraint(array, pltpu.HBM)
        else:
            spec = pl.BlockSpec(memory_space=pl.ANY)
        args.append(array)
        in_specs.append(spec)
    out_specs = [
        pl.BlockSpec(memory_space=pl.ANY if isinstance(shape, jax.ShapeDtypeStruct) else pltpu.VMEM)
        for shape in outs.values()
    ]
    got = pl.pallas_call(
        kernel,
        out_shape=list(outs.values()),
        in_specs=in_specs,
        out_specs=out_specs,
        input_output_aliases={list(ins).index(a): list(outs).index(b) for a, b in aliases},
        scratch_shapes=list(scratch.values()),
        compiler_params=pltpu.CompilerParams(vmem_limit_bytes=VMEM_LIMIT),
        cost_estimate=pl.CostEstimate(flops=FLOPS, bytes_accessed=1024, transcendentals=0),
        name=name,
    )(*args)
    return dict(zip(outs, got))


FLOPS = 2 * 10**10


class Gather:
    def __init__(self, sizes, refs, out, flip, rows, cols, sem):
        self.z, self.refs, self.out, self.flip, self.rows, self.cols = sizes, refs, refs[out], flip, rows, cols
        self.sem = sem

    def start(self):
        z, refs = self.z, self.refs
        cols, b = refs[self.cols + "_s"], refs["b"]
        base = (refs["info"][0] ^ self.flip) * z.half
        first, last = self.rows

        def one_row(i, _):
            for m in range(z.ra):
                at = pl.multiple_of(((i - first) * z.ra + m) * z.bs, z.bs)
                source = b.at[cols[m, base + i]]
                pltpu.make_async_copy(source, self.out.at[pl.ds(at, z.bs)], self.sem).start()
            return 0

        lax.fori_loop(first, last, one_row, 0, unroll=2)

    def finish(self):
        z, refs = self.z, self.refs
        table, cols = refs["table"], refs[self.cols + "_v"][...]
        kw = table.shape[1]
        both = [entries(cols, h * z.half, z.half, z.rb) for h in range(2)]
        odd = (refs["info"][0] ^ self.flip) == 1
        named = jnp.where(odd, both[1], both[0])
        named = jnp.broadcast_to(named, (kw, named.shape[1]))
        picked = lax.broadcasted_iota(I32, named.shape, 0) == named
        picked = jnp.where(picked, 1.0, 0.0).astype(BF16)
        found = jnp.dot(table[...], picked, preferred_element_type=F32)
        slot = lax.broadcasted_iota(I32, (1, found.shape[1]), 1) // (z.ra * z.half)
        parts = []
        for part in range(PARTS):
            value = found[part * z.rb : part * z.rb + 1]
            for n in range(1, z.rb):
                value = jnp.where(slot == n, found[part * z.rb + n : part * z.rb + n + 1], value)
            parts.append(value)
        size = (self.rows[1] - self.rows[0]) * z.wide
        self.out[pl.ds(size, META), :] = stacked(parts, META).astype(BF16)
        blocks = self.out.at[pl.ds(0, size)]
        pltpu.make_async_copy(blocks, blocks, self.sem).wait()


class Add:
    def __init__(self, sizes, refs, a, b, rows):
        self.z, self.refs, self.a, self.b, self.rows = sizes, refs, a, b, rows

    @staticmethod
    def scratch(sizes, rows):
        return {
            "prod": pltpu.VMEM(((rows[1] - rows[0]) * sizes.wide, LANES), F32),
            "scl_v": pltpu.VMEM((8, LANES), F32),
            "col_v": pltpu.VMEM((8, LANES), I32),
            "scl_s": pltpu.SMEM((8, LANES), F32),
            "col_s": pltpu.SMEM((8, LANES), I32),
            "add_sems": pltpu.SemaphoreType.DMA((2,)),
        }

    def start(self):
        z, refs, a, b = self.z, self.refs, self.a, self.b
        first, last = self.rows
        scl_v, col_v = refs["scl_v"], refs["col_v"]
        a_meta = a[pl.ds(a.shape[0] - META, META), :].astype(F32)
        b_meta = b[pl.ds(b.shape[0] - META, META), :].astype(F32)
        scl_a = a_meta[0:1] + a_meta[1:2] + a_meta[2:3]
        scl_b = b_meta[0:1] + b_meta[1:2] + b_meta[2:3]
        scl_v[...] = jnp.broadcast_to(scl_a * scl_b, scl_v.shape)
        col_v[...] = jnp.broadcast_to((b_meta[3:4] * 256.0 + b_meta[4:5]).astype(I32), col_v.shape)
        sems = refs["add_sems"]
        self.moves = [
            pltpu.make_async_copy(scl_v, refs["scl_s"], sems.at[0]),
            pltpu.make_async_copy(col_v, refs["col_s"], sems.at[1]),
        ]
        for move in self.moves:
            move.start()
        row_block = lax.broadcasted_iota(I32, (z.wide, z.wide), 0) // z.bs
        col_block = lax.broadcasted_iota(I32, (z.wide, z.wide), 1) // z.bs
        diagonal = jnp.where(row_block == col_block, 1.0, 0.0).astype(BF16)
        for i in range(first, last):
            left = a[pl.ds(i * z.bs, z.bs), :]
            left = jnp.concatenate([left] * z.ra, axis=0) * diagonal
            rows = pl.ds((i - first) * z.wide, z.wide)
            refs["prod"][rows, :] = jnp.dot(left, b[rows, :], preferred_element_type=F32)

    def finish(self):
        z, refs = self.z, self.refs
        first, last = self.rows
        acc, prod, scl_s, col_s = refs["acc"], refs["prod"], refs["scl_s"], refs["col_s"]
        per = LANES // z.bs
        for move in self.moves:
            move.wait()
        lane_block = lax.broadcasted_iota(I32, (z.bs, LANES), 1) // z.bs

        for i in range(first, last):
            for m in range(z.ra):
                value = prod[pl.ds(((i - first) * z.ra + m) * z.bs, z.bs), :]
                placed = []
                for n in range(z.rb):
                    entry = (n * z.ra + m) * z.half + i
                    column = col_s[0, entry]
                    place = column & (per - 1)
                    moved = pltpu.roll(value, ((place - n) & (per - 1)) * z.bs, 1)
                    moved = jnp.where(lane_block == place, moved * scl_s[0, entry], 0.0)
                    placed.append((column // per, moved))
                for tile, moved in placed:
                    acc[i, tile] = acc[i, tile] + moved


def clear(acc):
    for i in range(acc.shape[0]):

        def clear_tile(tile, _, i=i):
            acc[i, tile] = jnp.zeros(acc.shape[2:], F32)
            return 0

        lax.fori_loop(0, acc.shape[1], clear_tile, 0, unroll=8)


def write_out(sizes, refs, rows):
    acc, stage, sems, out = refs["acc"], refs["stage"], refs["out_sems"], refs["out"]
    slots = stage.shape[0]
    tiles = sizes.tiles // CHUNKS
    pieces = [(i, chunk) for i in range(*rows) for chunk in range(CHUNKS)]

    def send(at):
        i, chunk = pieces[at]
        columns = pl.ds(chunk * tiles * LANES, tiles * LANES)
        return pltpu.make_async_copy(stage.at[at % slots], out.at[i, :, columns], sems.at[at % slots])

    for at, (i, chunk) in enumerate(pieces):
        if at >= slots:
            send(at - slots).wait()
        for tile in range(tiles):
            stage[at % slots, :, pl.ds(tile * LANES, LANES)] = acc[i, chunk * tiles + tile].astype(BF16)
        send(at).start()
    for at in range(max(0, len(pieces) - slots), len(pieces)):
        send(at).wait()


def first_answers(z, info, cols, b_scl, b_pos, b, rows, after):
    rb, kw = b_scl.shape

    def body(refs):
        answers = [
            Gather(z, refs, f"message{flip}", flip, rows, "cols", refs["sems"].at[flip]) for flip in range(2)
        ]
        moves = [
            pltpu.make_async_copy(refs["b_scl"], refs["scl"], refs["sems"].at[2]),
            pltpu.make_async_copy(refs["b_pos"], refs["pos"], refs["sems"].at[3]),
        ]
        for move in moves:
            move.start()
        for answer in answers:
            answer.start()
        for move in moves:
            move.wait()
        scale, column = refs["scl"][...], refs["pos"][...]
        table = three_parts(scale) + [(column >> 8).astype(F32), (column & 255).astype(F32)]
        table.append(jnp.zeros((refs["table"].shape[0] - PARTS * rb, kw), F32))
        refs["table"][...] = jnp.concatenate(table, axis=0).astype(BF16)
        for answer in answers:
            answer.finish()

    ins = {
        "info": (info, "smem"),
        "cols_s": (cols, "smem"),
        "cols_v": (cols, "vmem"),
        "b_scl": (b_scl, "hbm"),
        "b_pos": (b_pos, "hbm"),
        "b": (b, "hbm"),
    }
    ins.update({f"after{at}": (array, "any") for at, array in enumerate(after)})
    return kernel_call(
        "first_answers",
        body,
        ins,
        {
            "table": pltpu.VMEM((-(-PARTS * rb // 16) * 16, kw), BF16),
            "message0": z.message(rows),
            "message1": z.message(rows),
        },
        scratch={
            "scl": pltpu.VMEM(b_scl.shape, F32),
            "pos": pltpu.VMEM(b_pos.shape, I32),
            "sems": pltpu.SemaphoreType.DMA((4,)),
        },
    )


def split(z, info, a, a_scl, after):
    def body(refs):
        scale = refs["a_scl"][...]
        both = [entries(scale, h * z.half, z.half, z.rb) for h in range(2)]
        size = z.half * z.bs
        for flip, out in enumerate((refs["kept"], refs["given"])):
            side = refs["info"][0] ^ flip
            out[0, pl.ds(0, size), :] = refs["a"][pl.ds(pl.multiple_of(side * size, size), size), :]
            parts = three_parts(jnp.where(side == 1, both[1], both[0]))
            out[0, pl.ds(size, META), :] = stacked(parts, META).astype(BF16)

    piece = pltpu.VMEM((1, z.half * z.bs + META, z.wide), BF16)
    return kernel_call(
        "split",
        body,
        {"info": (info, "smem"), "a": (a, "vmem"), "a_scl": (a_scl, "vmem"), "after": (after, "any")},
        {"kept": piece, "given": piece},
    )


def join(own, taken):
    count = own.shape[0]

    def body(refs):
        refs["both"][pl.ds(0, count)] = refs["own"][...]
        refs["both"][pl.ds(count, count)] = refs["taken"][...]

    outs = {"both": pltpu.VMEM((2 * count,) + own.shape[1:], BF16)}
    return kernel_call("join", body, {"own": (own, "vmem"), "taken": (taken, "vmem")}, outs)["both"]


def more_answers(z, info, cols, table, b, rows, after):
    def body(refs):
        answers = [
            Gather(z, refs, f"message{flip}", flip, rows, "cols", refs["sems"].at[flip]) for flip in range(2)
        ]
        for answer in answers:
            answer.start()
        for answer in answers:
            answer.finish()

    return kernel_call(
        "more_answers",
        body,
        {
            "info": (info, "smem"),
            "cols_s": (cols, "smem"),
            "cols_v": (cols, "vmem"),
            "table": (table, "vmem"),
            "b": (b, "hbm"),
            "after": (after, "any"),
        },
        {"message0": z.message(rows), "message1": z.message(rows)},
        scratch={"sems": pltpu.SemaphoreType.DMA((2,))},
    )


def own_blocks(z, info, cols, table, b, rows, kept, after):
    def body(refs):
        answer = Gather(z, refs, "message", 1, rows, "cols", refs["sems"].at[0])
        local = Gather(z, refs, "local", 0, rows, "cols", refs["sems"].at[1])
        local.start()
        answer.start()
        clear(refs["acc"])
        local.finish()
        add = Add(z, refs, refs["kept"].at[0], refs["local"], rows)
        add.start()
        answer.finish()
        add.finish()

    return kernel_call(
        "own_blocks",
        body,
        {
            "info": (info, "smem"),
            "cols_s": (cols, "smem"),
            "cols_v": (cols, "vmem"),
            "table": (table, "vmem"),
            "b": (b, "hbm"),
            "kept": (kept, "vmem"),
            "after": (after, "any"),
        },
        {"acc": z.window(), "message": z.message(rows)},
        scratch={
            "sems": pltpu.SemaphoreType.DMA((2,)),
            "local": z.message(rows),
            **Add.scratch(z, rows),
        },
    )


def add_message(z, info, left, by, flip, message, rows, acc, answers=(), table=None, b=None, write=False, out=None, after=()):
    ins = {
        "info": (info, "smem"),
        "left": (left, "vmem"),
        "arrived": (message, "vmem"),
        "acc_in": (acc, "vmem"),
    }
    outs = {"acc": z.window()}
    aliases = [("acc_in", "acc")]
    scratch = Add.scratch(z, rows)
    if answers:
        ins.update(table=(table, "vmem"), b=(b, "hbm"))
        scratch["sems"] = pltpu.SemaphoreType.DMA((len(answers),))
    for at, (cols, _, span) in enumerate(answers):
        ins[f"cols{at}_s"] = (cols, "smem")
        ins[f"cols{at}_v"] = (cols, "vmem")
        outs[f"message{at}"] = z.message(span)
    ins.update({f"after{at}": (array, "any") for at, array in enumerate(after)})
    if write:
        outs["out"] = jax.ShapeDtypeStruct((z.half, z.bs, JW * z.bs), BF16)
        scratch["stage"] = pltpu.VMEM((8, z.bs, JW * z.bs // CHUNKS), BF16)
        scratch["out_sems"] = pltpu.SemaphoreType.DMA((8,))
        if out is not None:
            ins["out_in"] = (out, "any")
            aliases.append(("out_in", "out"))

    def body(refs):
        gathers = [
            Gather(z, refs, f"message{at}", side, span, f"cols{at}", refs["sems"].at[at])
            for at, (_, side, span) in enumerate(answers)
        ]
        for gather in gathers:
            gather.start()
        place = flip if by == 0 else refs["info"][1 + by] * 2 + flip
        add = Add(z, refs, refs["left"].at[place], refs["arrived"], rows)
        add.start()
        for gather in gathers:
            gather.finish()
        add.finish()
        if write:
            write_out(z, refs, rows)

    got = kernel_call("add_message", body, ins, outs, aliases, scratch)
    return got["acc"], [got[f"message{at}"] for at in range(len(answers))], got.get("out")


def on_device(a_blocks, a_scale, a_cols, b_blocks, b_scale, b_cols):
    panels = lax.axis_size("row")
    columns = lax.axis_size("col")
    halves = columns // panels
    a_part, a_scl, a_pos = a_blocks[0, 0], a_scale[0, 0].T, a_cols[0, 0].T
    b_part = b_blocks[0, 0]
    b_scl, b_pos = b_scale[0, 0].T, b_cols[0, 0].T
    nrows, bs, _ = a_part.shape
    half = nrows // halves
    z = Sizes(half, a_scl.shape[0], b_scl.shape[0], bs)
    row = lax.axis_index("row")
    parity = lax.axis_index("col") % halves
    info = jnp.stack([parity] + [row ^ ((row - by) % panels) for by in range(panels)]).astype(I32)

    def step(value, by, flip):
        pairs = [
            (c, ((c // halves + by) % panels) * halves + (c % halves ^ flip)) for c in range(columns)
        ]
        return lax.ppermute(value, "col", pairs)

    def named_by(by):
        pairs = []
        for r in range(panels):
            for c in range(columns):
                to_row = (r + by) % panels
                to_col = (c - halves * by) % columns
                pairs.append((r * columns + c, to_row * columns + to_col))
        return lax.ppermute(a_pos, ("row", "col"), pairs)

    order = sorted(range(1, panels), key=lambda by: -min(by, panels - by))
    every = (0, half)
    early = (0, half - max(1, half // 4))
    late = (early[1], half)
    last = order[-1]
    asked = {by: named_by(by) for by in order}

    got = first_answers(
        z, info, asked[order[0]], b_scl, b_pos, b_part, every, [asked[by] for by in order[1:]]
    )
    table = got["table"]
    moving = {(order[0], flip): step(got[f"message{flip}"], order[0], flip) for flip in range(halves)}
    pieces = split(z, info, a_part.reshape(nrows * bs, z.wide), a_scl, got["message0"])
    own_left = join(pieces["kept"], step(pieces["given"], 0, 1))
    left = own_left
    bit = 1
    while bit < panels:
        left = join(left, lax.ppermute(left, "row", [(r, r ^ bit) for r in range(panels)]))
        bit *= 2
    after = got["message0"]
    for by in order[1:-1]:
        got = more_answers(z, info, asked[by], table, b_part, every, after)
        after = got["message0"]
        for flip in range(halves):
            moving[by, flip] = step(got[f"message{flip}"], by, flip)

    mine = own_blocks(z, info, a_pos, table, b_part, every, pieces["kept"], after)
    taken = step(mine["message"], 0, 1)
    more = {"table": table, "b": b_part}
    acc, answers, _ = add_message(
        z, info, own_left, 0, 1, taken, every, mine["acc"], [(asked[last], 0, every)], **more
    )
    ends = answers
    for by in order[:-1]:
        for flip in range(halves):
            first = by == order[0]
            acc, answers, _ = add_message(
                z, info, left, by, flip, moving[by, flip], every, acc,
                [(asked[last], 1, late if flip else early)] if first else [],
                after=ends[-1:] if first else [], **(more if first else {}),
            )
            ends += answers
    acc = add_message(z, info, left, last, 0, step(ends[0], last, 0), every, acc)[0]
    acc, _, out = add_message(z, info, left, last, 1, step(ends[1], last, 1), early, acc, write=True)
    out = add_message(z, info, left, last, 1, step(ends[2], last, 1), late, acc, write=True, out=out)[2]
    return out[None, None]


def solution(mesh):
    in_specs = (
        P("col", "row", None, None, None),
        P("col", "row", None, None),
        P("col", "row", None, None),
        P("col", "row", None, None, None),
        P("col", "row", None, None),
        P("col", "row", None, None),
    )
    out_specs = P("col", "row", None, None, None)
    return jax.shard_map(
        on_device, mesh=mesh, in_specs=in_specs, out_specs=out_specs, check_vma=False
    )
```

```python
import functools

import jax
import jax.numpy as jnp
from jax import lax
from jax.experimental import pallas as pl
from jax.experimental.pallas import tpu as pltpu
from jax.sharding import PartitionSpec as P

JW = 512
LANES = 128
META = 16
PARTS = 5
CHUNKS = 4
F32, BF16, I32 = jnp.float32, jnp.bfloat16, jnp.int32
VMEM_LIMIT = 12 * 1024 * 1024


def three_parts(x):
    high = x.astype(BF16).astype(F32)
    rest = x - high
    mid = rest.astype(BF16).astype(F32)
    return [high, mid, (rest - mid).astype(BF16).astype(F32)]


def stacked(parts, rows):
    which = lax.broadcasted_iota(I32, (rows, parts[0].shape[1]), 0)
    tile = jnp.zeros(which.shape, F32)
    for at, part in enumerate(parts):
        tile = jnp.where(which == at, jnp.broadcast_to(part, which.shape), tile)
    return tile


def entries(values, first, half, rb):
    ra = values.shape[0]
    one = [values[m : m + 1, first : first + half] for m in range(ra)]
    return jnp.concatenate(one * rb, axis=1)


class Sizes:
    def __init__(self, half, ra, rb, bs):
        self.half, self.ra, self.rb, self.bs = half, ra, rb, bs
        self.wide = ra * bs
        self.tiles = JW * bs // LANES

    def message(self, rows):
        return pltpu.VMEM(((rows[1] - rows[0]) * self.wide + META, self.rb * self.bs), BF16)

    def window(self):
        return pltpu.VMEM((self.half, self.tiles, self.bs, LANES), F32)


def kernel_call(name, body, ins, outs, aliases=(), scratch=None):
    scratch = scratch or {}
    names = list(ins) + list(outs) + list(scratch)

    def kernel(*refs):
        body(dict(zip(names, refs)))

    args, in_specs = [], []
    for array, place in ins.values():
        if place == "smem":
            spec = pl.BlockSpec(memory_space=pltpu.SMEM)
        elif place == "vmem":
            spec = pl.BlockSpec(memory_space=pltpu.VMEM)
            array = pltpu.with_memory_space_constraint(array, pltpu.VMEM)
        elif place == "hbm":
            spec = pl.BlockSpec(memory_space=pltpu.HBM)
            array = pltpu.with_memory_space_constraint(array, pltpu.HBM)
        else:
            spec = pl.BlockSpec(memory_space=pl.ANY)
        args.append(array)
        in_specs.append(spec)
    out_specs = [
        pl.BlockSpec(memory_space=pl.ANY if isinstance(shape, jax.ShapeDtypeStruct) else pltpu.VMEM)
        for shape in outs.values()
    ]
    got = pl.pallas_call(
        kernel,
        out_shape=list(outs.values()),
        in_specs=in_specs,
        out_specs=out_specs,
        input_output_aliases={list(ins).index(a): list(outs).index(b) for a, b in aliases},
        scratch_shapes=list(scratch.values()),
        compiler_params=pltpu.CompilerParams(vmem_limit_bytes=VMEM_LIMIT),
        cost_estimate=pl.CostEstimate(flops=FLOPS, bytes_accessed=1024, transcendentals=0),
        name=name,
    )(*args)
    return dict(zip(outs, got))


FLOPS = 2 * 10**10


class Gather:
    def __init__(self, sizes, refs, out, flip, rows, cols, sem):
        self.z, self.refs, self.out, self.flip, self.rows, self.cols = sizes, refs, refs[out], flip, rows, cols
        self.sem = sem

    def start(self):
        z, refs = self.z, self.refs
        cols, b = refs[self.cols[0] + "_s"].at[self.cols[1]], refs["b"]
        base = (refs["info"][0] ^ self.flip) * z.half
        first, last = self.rows

        def one_row(i, _):
            for m in range(z.ra):
                at = pl.multiple_of(((i - first) * z.ra + m) * z.bs, z.bs)
                source = b.at[cols[m, base + i]]
                pltpu.make_async_copy(source, self.out.at[pl.ds(at, z.bs)], self.sem).start()
            return 0

        lax.fori_loop(first, last, one_row, 0, unroll=2)

    def finish(self):
        z, refs = self.z, self.refs
        table, cols = refs["table"], refs[self.cols[0] + "_v"][self.cols[1]]
        kw = table.shape[1]
        both = [entries(cols, h * z.half, z.half, z.rb) for h in range(2)]
        odd = (refs["info"][0] ^ self.flip) == 1
        named = jnp.where(odd, both[1], both[0])
        named = jnp.broadcast_to(named, (kw, named.shape[1]))
        picked = lax.broadcasted_iota(I32, named.shape, 0) == named
        picked = jnp.where(picked, 1.0, 0.0).astype(BF16)
        found = jnp.dot(table[...], picked, preferred_element_type=F32)
        slot = lax.broadcasted_iota(I32, (1, found.shape[1]), 1) // (z.ra * z.half)
        parts = []
        for part in range(PARTS):
            value = found[part * z.rb : part * z.rb + 1]
            for n in range(1, z.rb):
                value = jnp.where(slot == n, found[part * z.rb + n : part * z.rb + n + 1], value)
            parts.append(value)
        size = (self.rows[1] - self.rows[0]) * z.wide
        self.out[pl.ds(size, META), :] = stacked(parts, META).astype(BF16)
        blocks = self.out.at[pl.ds(0, size)]
        pltpu.make_async_copy(blocks, blocks, self.sem).wait()


class Add:
    def __init__(self, sizes, refs, a, b, rows):
        self.z, self.refs, self.a, self.b, self.rows = sizes, refs, a, b, rows

    @staticmethod
    def scratch(sizes, rows):
        return {
            "prod": pltpu.VMEM(((rows[1] - rows[0]) * sizes.wide, LANES), F32),
            "scl_v": pltpu.VMEM((8, LANES), F32),
            "col_v": pltpu.VMEM((8, LANES), I32),
            "scl_s": pltpu.SMEM((8, LANES), F32),
            "col_s": pltpu.SMEM((8, LANES), I32),
            "add_sems": pltpu.SemaphoreType.DMA((2,)),
        }

    def start(self):
        z, refs, a, b = self.z, self.refs, self.a, self.b
        first, last = self.rows
        scl_v, col_v = refs["scl_v"], refs["col_v"]
        a_meta = a[pl.ds(a.shape[0] - META, META), :].astype(F32)
        b_meta = b[pl.ds(b.shape[0] - META, META), :].astype(F32)
        scl_a = a_meta[0:1] + a_meta[1:2] + a_meta[2:3]
        scl_b = b_meta[0:1] + b_meta[1:2] + b_meta[2:3]
        scl_v[...] = jnp.broadcast_to(scl_a * scl_b, scl_v.shape)
        col_v[...] = jnp.broadcast_to((b_meta[3:4] * 256.0 + b_meta[4:5]).astype(I32), col_v.shape)
        sems = refs["add_sems"]
        self.moves = [
            pltpu.make_async_copy(scl_v, refs["scl_s"], sems.at[0]),
            pltpu.make_async_copy(col_v, refs["col_s"], sems.at[1]),
        ]
        for move in self.moves:
            move.start()
        row_block = lax.broadcasted_iota(I32, (z.wide, z.wide), 0) // z.bs
        col_block = lax.broadcasted_iota(I32, (z.wide, z.wide), 1) // z.bs
        diagonal = jnp.where(row_block == col_block, 1.0, 0.0).astype(BF16)
        for i in range(first, last):
            left = a[pl.ds(i * z.bs, z.bs), :]
            left = jnp.concatenate([left] * z.ra, axis=0) * diagonal
            rows = pl.ds((i - first) * z.wide, z.wide)
            refs["prod"][rows, :] = jnp.dot(left, b[rows, :], preferred_element_type=F32)

    def finish(self, writer=None):
        z, refs = self.z, self.refs
        first, last = self.rows
        acc, prod, scl_s, col_s = refs["acc"], refs["prod"], refs["scl_s"], refs["col_s"]
        per = LANES // z.bs
        for move in self.moves:
            move.wait()
        lane_block = lax.broadcasted_iota(I32, (z.bs, LANES), 1) // z.bs

        for i in range(first, last):
            for m in range(z.ra):
                value = prod[pl.ds(((i - first) * z.ra + m) * z.bs, z.bs), :]
                placed = []
                for n in range(z.rb):
                    entry = (n * z.ra + m) * z.half + i
                    column = col_s[0, entry]
                    place = column & (per - 1)
                    moved = pltpu.roll(value, ((place - n) & (per - 1)) * z.bs, 1)
                    moved = jnp.where(lane_block == place, moved * scl_s[0, entry], 0.0)
                    placed.append((column // per, moved))
                for tile, moved in placed:
                    acc[i, tile] = acc[i, tile] + moved
            if writer is not None:
                writer.row(i)
        if writer is not None:
            writer.finish()


class Writer:
    def __init__(self, sizes, refs):
        self.z, self.refs, self.sent = sizes, refs, []

    def send(self, at):
        stage, (i, chunk) = self.refs["stage"], self.sent[at]
        slot = at % stage.shape[0]
        width = stage.shape[2]
        there = self.refs["out"].at[i, :, pl.ds(chunk * width, width)]
        return pltpu.make_async_copy(stage.at[slot], there, self.refs["out_sems"].at[slot])

    def row(self, i):
        acc, stage = self.refs["acc"], self.refs["stage"]
        slots, tiles = stage.shape[0], self.z.tiles // CHUNKS
        for chunk in range(CHUNKS):
            at = len(self.sent)
            if at >= slots:
                self.send(at - slots).wait()
            for tile in range(tiles):
                piece = acc[i, chunk * tiles + tile].astype(BF16)
                stage[at % slots, :, pl.ds(tile * LANES, LANES)] = piece
            self.sent.append((i, chunk))
            self.send(at).start()

    def finish(self):
        for at in range(max(0, len(self.sent) - self.refs["stage"].shape[0]), len(self.sent)):
            self.send(at).wait()


def clear(acc):
    for i in range(acc.shape[0]):

        def clear_tile(tile, _, i=i):
            acc[i, tile] = jnp.zeros(acc.shape[2:], F32)
            return 0

        lax.fori_loop(0, acc.shape[1], clear_tile, 0, unroll=8)


def first_answers(z, info, own_cols, cols, b_scl, b_pos, b, rows):
    rb, kw = b_scl.shape

    def body(refs):
        answers = [
            Gather(z, refs, f"message{flip}", flip, rows, ("cols", 0), refs["sems"].at[flip])
            for flip in range(2)
        ]
        moves = [
            pltpu.make_async_copy(refs["b_scl"], refs["scl"], refs["sems"].at[2]),
            pltpu.make_async_copy(refs["b_pos"], refs["pos"], refs["sems"].at[3]),
        ]
        for move in moves:
            move.start()
        for answer in answers:
            answer.start()
        refs["both"][pl.ds(0, 1)] = refs["own_v"][...]
        refs["both"][pl.ds(1, 1)] = refs["cols_v"][...]
        for move in moves:
            move.wait()
        scale, column = refs["scl"][...], refs["pos"][...]
        table = three_parts(scale) + [(column >> 8).astype(F32), (column & 255).astype(F32)]
        table.append(jnp.zeros((refs["table"].shape[0] - PARTS * rb, kw), F32))
        refs["table"][...] = jnp.concatenate(table, axis=0).astype(BF16)
        for answer in answers:
            answer.finish()

    ins = {
        "info": (info, "smem"),
        "cols_s": (cols, "smem"),
        "cols_v": (cols, "vmem"),
        "own_v": (own_cols, "vmem"),
        "b_scl": (b_scl, "hbm"),
        "b_pos": (b_pos, "hbm"),
        "b": (b, "hbm"),
    }
    return kernel_call(
        "first_answers",
        body,
        ins,
        {
            "table": pltpu.VMEM((-(-PARTS * rb // 16) * 16, kw), BF16),
            "message0": z.message(rows),
            "message1": z.message(rows),
            "both": pltpu.VMEM((2,) + cols.shape[1:], I32),
        },
        scratch={
            "scl": pltpu.VMEM(b_scl.shape, F32),
            "pos": pltpu.VMEM(b_pos.shape, I32),
            "sems": pltpu.SemaphoreType.DMA((4,)),
        },
    )


def split(z, info, a, a_scl, after):
    def body(refs):
        scale = refs["a_scl"][...]
        both = [entries(scale, h * z.half, z.half, z.rb) for h in range(2)]
        size = z.half * z.bs
        for flip, out in enumerate((refs["kept"], refs["given"])):
            side = refs["info"][0] ^ flip
            out[0, pl.ds(0, size), :] = refs["a"][pl.ds(pl.multiple_of(side * size, size), size), :]
            parts = three_parts(jnp.where(side == 1, both[1], both[0]))
            out[0, pl.ds(size, META), :] = stacked(parts, META).astype(BF16)

    piece = pltpu.VMEM((1, z.half * z.bs + META, z.wide), BF16)
    return kernel_call(
        "split",
        body,
        {"info": (info, "smem"), "a": (a, "vmem"), "a_scl": (a_scl, "vmem"), "after": (after, "any")},
        {"kept": piece, "given": piece},
    )


def join(own, taken):
    count = own.shape[0]

    def body(refs):
        refs["both"][pl.ds(0, count)] = refs["own"][...]
        refs["both"][pl.ds(count, count)] = refs["taken"][...]

    outs = {"both": pltpu.VMEM((2 * count,) + own.shape[1:], own.dtype)}
    return kernel_call("join", body, {"own": (own, "vmem"), "taken": (taken, "vmem")}, outs)["both"]


def more_answers(z, info, cols, which, table, b, rows, after):
    def body(refs):
        answers = [
            Gather(z, refs, f"message{flip}", flip, rows, ("cols", which), refs["sems"].at[flip])
            for flip in range(2)
        ]
        for answer in answers:
            answer.start()
        for answer in answers:
            answer.finish()

    return kernel_call(
        "more_answers",
        body,
        {
            "info": (info, "smem"),
            "cols_s": (cols, "smem"),
            "cols_v": (cols, "vmem"),
            "table": (table, "vmem"),
            "b": (b, "hbm"),
            "after": (after, "any"),
        },
        {"message0": z.message(rows), "message1": z.message(rows)},
        scratch={"sems": pltpu.SemaphoreType.DMA((2,))},
    )


def own_blocks(z, info, cols, table, b, rows, kept, after):
    def body(refs):
        answer = Gather(z, refs, "message", 1, rows, ("cols", 0), refs["sems"].at[0])
        local = Gather(z, refs, "local", 0, rows, ("cols", 0), refs["sems"].at[1])
        local.start()
        answer.start()
        clear(refs["acc"])
        local.finish()
        add = Add(z, refs, refs["kept"].at[0], refs["local"], rows)
        add.start()
        answer.finish()
        add.finish()

    return kernel_call(
        "own_blocks",
        body,
        {
            "info": (info, "smem"),
            "cols_s": (cols, "smem"),
            "cols_v": (cols, "vmem"),
            "table": (table, "vmem"),
            "b": (b, "hbm"),
            "kept": (kept, "vmem"),
            "after": (after, "any"),
        },
        {"acc": z.window(), "message": z.message(rows)},
        scratch={
            "sems": pltpu.SemaphoreType.DMA((2,)),
            "local": z.message(rows),
            **Add.scratch(z, rows),
        },
    )


def add_message(z, info, left, by, flip, message, rows, acc, answers=(), table=None, b=None, write=False, out=None, after=()):
    ins = {
        "info": (info, "smem"),
        "left": (left, "vmem"),
        "arrived": (message, "vmem"),
        "acc_in": (acc, "vmem"),
    }
    outs = {"acc": z.window()}
    aliases = [("acc_in", "acc")]
    scratch = Add.scratch(z, rows)
    if answers:
        ins.update(table=(table, "vmem"), b=(b, "hbm"))
        scratch["sems"] = pltpu.SemaphoreType.DMA((len(answers),))
    for at, (cols, _, _, span) in enumerate(answers):
        ins[f"cols{at}_s"] = (cols, "smem")
        ins[f"cols{at}_v"] = (cols, "vmem")
        outs[f"message{at}"] = z.message(span)
    ins.update({f"after{at}": (array, "any") for at, array in enumerate(after)})
    if write:
        outs["out"] = jax.ShapeDtypeStruct((z.half, z.bs, JW * z.bs), BF16)
        scratch["stage"] = pltpu.VMEM((8, z.bs, JW * z.bs // CHUNKS), BF16)
        scratch["out_sems"] = pltpu.SemaphoreType.DMA((8,))
        if out is not None:
            ins["out_in"] = (out, "any")
            aliases.append(("out_in", "out"))

    def body(refs):
        gathers = [
            Gather(z, refs, f"message{at}", side, span, (f"cols{at}", which), refs["sems"].at[at])
            for at, (_, which, side, span) in enumerate(answers)
        ]
        for gather in gathers:
            gather.start()
        place = flip if by == 0 else refs["info"][1 + by] * 2 + flip
        add = Add(z, refs, refs["left"].at[place], refs["arrived"], rows)
        add.start()
        for gather in gathers:
            gather.finish()
        add.finish(Writer(z, refs) if write else None)

    got = kernel_call("add_message", body, ins, outs, aliases, scratch)
    return got["acc"], [got[f"message{at}"] for at in range(len(answers))], got.get("out")


def on_device(a_blocks, a_scale, a_cols, b_blocks, b_scale, b_cols):
    panels = lax.axis_size("row")
    columns = lax.axis_size("col")
    halves = columns // panels
    a_part, a_scl, a_pos = a_blocks[0, 0], a_scale[0, 0].T, a_cols[0, 0].T
    b_part = b_blocks[0, 0]
    b_scl, b_pos = b_scale[0, 0].T, b_cols[0, 0].T
    nrows, bs, _ = a_part.shape
    half = nrows // halves
    z = Sizes(half, a_scl.shape[0], b_scl.shape[0], bs)
    row = lax.axis_index("row")
    parity = lax.axis_index("col") % halves
    info = jnp.stack([parity] + [row ^ ((row - by) % panels) for by in range(panels)]).astype(I32)

    def step(value, by, flip):
        pairs = [
            (c, ((c // halves + by) % panels) * halves + (c % halves ^ flip)) for c in range(columns)
        ]
        return lax.ppermute(value, "col", pairs)

    def named_by(by, cols):
        pairs = []
        for r in range(panels):
            for c in range(columns):
                to_row = (r + by) % panels
                to_col = (c - halves * by) % columns
                pairs.append((r * columns + c, to_row * columns + to_col))
        return lax.ppermute(cols, ("row", "col"), pairs)

    every = (0, half)
    order = sorted(range(1, panels), key=lambda by: -min(by, panels - by))
    last = order[-1]
    own_cols = a_pos[None]

    cols = named_by(order[0], own_cols)
    got = first_answers(z, info, own_cols, cols, b_scl, b_pos, b_part, every)
    table = got["table"]
    moving = {(order[0], flip): step(got[f"message{flip}"], order[0], flip) for flip in range(halves)}

    asked, known, by = {0: (own_cols, 0)}, [0, order[0]], panels // 4
    cols = got["both"]
    while by:
        more_cols = named_by(by, cols)
        asked.update({(to + by) % panels: (more_cols, at) for at, to in enumerate(known)})
        known += [(to + by) % panels for to in known]
        by //= 2
        if by:
            cols = join(cols, more_cols)

    pieces = split(z, info, a_part.reshape(nrows * bs, z.wide), a_scl, got["message0"])
    own_left = join(pieces["kept"], step(pieces["given"], 0, 1))
    left = own_left
    bit = 1
    while bit < panels:
        left = join(left, lax.ppermute(left, "row", [(r, r ^ bit) for r in range(panels)]))
        bit *= 2

    mine = own_blocks(z, info, own_cols, table, b_part, every, pieces["kept"], got["message0"])
    taken = step(mine["message"], 0, 1)
    after = mine["message"]
    for by in order[1:-1]:
        got = more_answers(z, info, *asked[by], table, b_part, every, after)
        after = got["message0"]
        for flip in range(halves):
            moving[by, flip] = step(got[f"message{flip}"], by, flip)

    more = {"table": table, "b": b_part}
    acc, answers, _ = add_message(
        z, info, own_left, 0, 1, taken, every, mine["acc"], [(*asked[last], 0, every)],
        after=[after], **more
    )
    ends = answers
    for by in order[:-1]:
        for flip in range(halves):
            first = by == order[0] and flip == 0
            acc, answers, _ = add_message(
                z, info, left, by, flip, moving[by, flip], every, acc,
                [(*asked[last], 1, every)] if first else [],
                after=ends[-1:] if first else [], **(more if first else {}),
            )
            ends += answers
    acc = add_message(z, info, left, last, 0, step(ends[0], last, 0), every, acc)[0]
    out = add_message(z, info, left, last, 1, step(ends[1], last, 1), every, acc, write=True)[2]
    return out[None, None]


def solution(mesh):
    in_specs = (
        P("col", "row", None, None, None),
        P("col", "row", None, None),
        P("col", "row", None, None),
        P("col", "row", None, None, None),
        P("col", "row", None, None),
        P("col", "row", None, None),
    )
    out_specs = P("col", "row", None, None, None)
    return jax.shard_map(
        on_device, mesh=mesh, in_specs=in_specs, out_specs=out_specs, check_vma=False
    )
```

```python
import types

import jax
import jax.numpy as jnp
from jax import lax
from jax.experimental import pallas as pl
from jax.experimental.pallas import tpu as pltpu
from jax.sharding import PartitionSpec as P

JW = 512
LANES = 128
META = 16
PARTS = 5
CHUNKS = 4
SLOTS = 8
ROW, COL = "row", "col"
F32, BF16, I32 = jnp.float32, jnp.bfloat16, jnp.int32
VMEM_LIMIT = 12 * 1024 * 1024
SMEM, VMEM, HBM, ANY = pltpu.SMEM, pltpu.VMEM, pltpu.HBM, pl.ANY
DMA = pltpu.SemaphoreType.DMA
copy = pltpu.make_async_copy


def three_parts(x):
    high = x.astype(BF16).astype(F32)
    rest = x - high
    mid = rest.astype(BF16).astype(F32)
    return [high, mid, (rest - mid).astype(BF16).astype(F32)]


def stacked(parts, rows):
    which = lax.broadcasted_iota(I32, (rows, parts[0].shape[1]), 0)
    tile = jnp.zeros(which.shape, F32)
    for at, part in enumerate(parts):
        tile = jnp.where(which == at, jnp.broadcast_to(part, which.shape), tile)
    return tile


def entries(values, first, half, rb):
    ra = values.shape[0]
    one = [values[m : m + 1, first : first + half] for m in range(ra)]
    return jnp.concatenate(one * rb, axis=1)


class Sizes:
    def __init__(self, half, ra, rb, bs):
        self.half, self.ra, self.rb, self.bs = half, ra, rb, bs
        self.wide = ra * bs
        self.tiles = JW * bs // LANES

    def message(self):
        return VMEM((self.half * self.wide + META, self.rb * self.bs), BF16)

    def window(self):
        return VMEM((self.half, self.tiles, self.bs, LANES), F32)


class In:
    def __init__(self, array, place):
        self.array, self.place = array, place
        if place in (VMEM, HBM):
            self.array = pltpu.with_memory_space_constraint(array, place)


def kernel_call(name, body, ins, outs, aliases=(), scratch=None):
    names = list(ins) + list(outs) + list(scratch or {})

    def kernel(*refs):
        body(types.SimpleNamespace(**dict(zip(names, refs))))

    def out_place(shape):
        return ANY if isinstance(shape, jax.ShapeDtypeStruct) else VMEM

    got = pl.pallas_call(
        kernel,
        out_shape=list(outs.values()),
        in_specs=[pl.BlockSpec(memory_space=one.place) for one in ins.values()],
        out_specs=[pl.BlockSpec(memory_space=out_place(shape)) for shape in outs.values()],
        input_output_aliases={list(ins).index(a): list(outs).index(b) for a, b in aliases},
        scratch_shapes=list((scratch or {}).values()),
        compiler_params=pltpu.CompilerParams(vmem_limit_bytes=VMEM_LIMIT),
        cost_estimate=pl.CostEstimate(flops=2 * 10**10, bytes_accessed=1024, transcendentals=0),
        name=name,
    )(*[one.array for one in ins.values()])
    return types.SimpleNamespace(**dict(zip(outs, got)))


class Gather:
    def __init__(self, z, refs, message, flip, which, sem):
        self.z, self.refs, self.message, self.flip, self.which, self.sem = z, refs, message, flip, which, sem

    def start(self):
        z, refs = self.z, self.refs
        cols = refs.cols_s.at[self.which]
        base = (refs.info[0] ^ self.flip) * z.half

        def one_row(i, _):
            for m in range(z.ra):
                at = pl.multiple_of((i * z.ra + m) * z.bs, z.bs)
                copy(refs.b.at[cols[m, base + i]], self.message.at[pl.ds(at, z.bs)], self.sem).start()
            return 0

        lax.fori_loop(0, z.half, one_row, 0, unroll=2)

    def finish(self):
        z, refs = self.z, self.refs
        table, cols = refs.table, refs.cols_v[self.which]
        kw = table.shape[1]
        both = [entries(cols, h * z.half, z.half, z.rb) for h in range(2)]
        named = jnp.where((refs.info[0] ^ self.flip) == 1, both[1], both[0])
        named = jnp.broadcast_to(named, (kw, named.shape[1]))
        picked = lax.broadcasted_iota(I32, named.shape, 0) == named
        picked = jnp.where(picked, 1.0, 0.0).astype(BF16)
        found = jnp.dot(table[...], picked, preferred_element_type=F32)
        slot = lax.broadcasted_iota(I32, (1, found.shape[1]), 1) // (z.ra * z.half)
        parts = []
        for part in range(PARTS):
            value = found[part * z.rb : part * z.rb + 1]
            for n in range(1, z.rb):
                value = jnp.where(slot == n, found[part * z.rb + n : part * z.rb + n + 1], value)
            parts.append(value)
        size = z.half * z.wide
        self.message[pl.ds(size, META), :] = stacked(parts, META).astype(BF16)
        blocks = self.message.at[pl.ds(0, size)]
        copy(blocks, blocks, self.sem).wait()


def add_scratch(z, count=1):
    return dict(
        prods=VMEM((count, z.half * z.wide, LANES), F32),
        scl_v=VMEM((8, LANES), F32),
        col_v=VMEM((8, LANES), I32),
        scl_s=SMEM((8, LANES), F32),
        col_s=SMEM((8, LANES), I32),
        add_sems=DMA((2,)),
    )


class Add:
    def __init__(self, z, refs, pairs):
        self.z, self.refs, self.pairs = z, refs, pairs

    def start(self):
        z, refs = self.z, self.refs
        for at, (a, b) in enumerate(self.pairs):
            a_meta = a[pl.ds(a.shape[0] - META, META), :].astype(F32)
            b_meta = b[pl.ds(b.shape[0] - META, META), :].astype(F32)
            scl_a = a_meta[0:1] + a_meta[1:2] + a_meta[2:3]
            scl_b = b_meta[0:1] + b_meta[1:2] + b_meta[2:3]
            refs.scl_v[at : at + 1, :] = scl_a * scl_b
            refs.col_v[at : at + 1, :] = (b_meta[3:4] * 256.0 + b_meta[4:5]).astype(I32)
        self.moves = [
            copy(refs.scl_v, refs.scl_s, refs.add_sems.at[0]),
            copy(refs.col_v, refs.col_s, refs.add_sems.at[1]),
        ]
        for move in self.moves:
            move.start()
        row_block = lax.broadcasted_iota(I32, (z.wide, z.wide), 0) // z.bs
        col_block = lax.broadcasted_iota(I32, (z.wide, z.wide), 1) // z.bs
        diagonal = jnp.where(row_block == col_block, 1.0, 0.0).astype(BF16)
        for at, (a, b) in enumerate(self.pairs):
            for i in range(z.half):
                left = a[pl.ds(i * z.bs, z.bs), :]
                left = jnp.concatenate([left] * z.ra, axis=0) * diagonal
                rows = pl.ds(i * z.wide, z.wide)
                refs.prods[at, rows, :] = jnp.dot(left, b[rows, :], preferred_element_type=F32)

    def finish(self, after_row=None):
        z, refs, acc = self.z, self.refs, self.refs.acc
        per = LANES // z.bs
        for move in self.moves:
            move.wait()
        lane_block = lax.broadcasted_iota(I32, (8, LANES), 1) // z.bs
        for i in range(z.half):
            for at in range(len(self.pairs)):
                for m in range(z.ra):
                    value = refs.prods[at, pl.ds((i * z.ra + m) * z.bs, z.bs), :]
                    placed = []
                    for n in range(z.rb):
                        entry = (n * z.ra + m) * z.half + i
                        column = refs.col_s[at, entry]
                        place = column & (per - 1)
                        moved = pltpu.roll(value, ((place - n) & (per - 1)) * z.bs, 1)
                        scale = jnp.where(lane_block == place, refs.scl_s[at, entry], 0.0)
                        placed.append((column // per, moved * jnp.concatenate([scale] * (z.bs // 8), axis=0)))
                    for tile, moved in placed:
                        acc[i, tile] = acc[i, tile] + moved
            if after_row is not None:
                after_row(i)


def clear(acc):
    for i in range(acc.shape[0]):

        def clear_tile(tile, _, i=i):
            acc[i, tile] = jnp.zeros(acc.shape[2:], F32)
            return 0

        lax.fori_loop(0, acc.shape[1], clear_tile, 0, unroll=8)


class WriteAll:
    def __init__(self, z, refs):
        self.z, self.refs, self.sent = z, refs, []

    @staticmethod
    def scratch(z):
        return dict(stage=VMEM((SLOTS, z.bs, JW * z.bs // CHUNKS), BF16), out_sems=DMA((SLOTS,)))

    def send(self, at):
        i, chunk = self.sent[at]
        slot, width = at % SLOTS, self.refs.stage.shape[2]
        there = self.refs.out.at[i, :, pl.ds(chunk * width, width)]
        return copy(self.refs.stage.at[slot], there, self.refs.out_sems.at[slot])

    def row(self, i):
        acc, stage = self.refs.acc, self.refs.stage
        tiles = self.z.tiles // CHUNKS
        for chunk in range(CHUNKS):
            at = len(self.sent)
            if at >= SLOTS:
                self.send(at - SLOTS).wait()
            for tile in range(tiles):
                piece = acc[i, chunk * tiles + tile].astype(BF16)
                stage[at % SLOTS, :, pl.ds(tile * LANES, LANES)] = piece
            self.sent.append((i, chunk))
            self.send(at).start()

    def finish(self):
        for at in range(max(0, len(self.sent) - SLOTS), len(self.sent)):
            self.send(at).wait()


def prepare(info, own_cols, b_scl, b_pos):
    rb, kw = b_scl.shape

    def body(refs):
        moves = [
            copy(refs.b_scl, refs.scl, refs.sems.at[0]),
            copy(refs.b_pos, refs.pos, refs.sems.at[1]),
            copy(refs.own_cols, refs.own, refs.sems.at[2]),
        ]
        for move in moves:
            move.start()
        for move in moves:
            move.wait()
        scale, column = refs.scl[...], refs.pos[...]
        table = three_parts(scale) + [(column >> 8).astype(F32), (column & 255).astype(F32)]
        table.append(jnp.zeros((refs.table.shape[0] - PARTS * rb, kw), F32))
        refs.table[...] = jnp.concatenate(table, axis=0).astype(BF16)

    return kernel_call(
        "prepare",
        body,
        dict(info=In(info, SMEM), own_cols=In(own_cols, HBM), b_scl=In(b_scl, HBM), b_pos=In(b_pos, HBM)),
        dict(table=VMEM((-(-PARTS * rb // 16) * 16, kw), BF16), own=VMEM(own_cols.shape, I32)),
        scratch=dict(scl=VMEM(b_scl.shape, F32), pos=VMEM(b_pos.shape, I32), sems=DMA((3,))),
    )


def split(z, info, a, a_scl, after, asked):
    def body(refs):
        scale = refs.a_scl[...]
        both = [entries(scale, h * z.half, z.half, z.rb) for h in range(2)]
        size = z.half * z.bs
        for flip, out in enumerate((refs.kept, refs.given)):
            side = refs.info[0] ^ flip
            out[0, pl.ds(0, size), :] = refs.a[pl.ds(pl.multiple_of(side * size, size), size), :]
            parts = three_parts(jnp.where(side == 1, both[1], both[0]))
            out[0, pl.ds(size, META), :] = stacked(parts, META).astype(BF16)

    piece = VMEM((1, z.half * z.bs + META, z.wide), BF16)
    return kernel_call(
        "split",
        body,
        dict(
            info=In(info, SMEM), a=In(a, VMEM), a_scl=In(a_scl, VMEM), after=In(after, ANY), asked=In(asked, ANY)
        ),
        dict(kept=piece, given=piece),
    )


def join(own, taken):
    count = own.shape[0]

    def body(refs):
        refs.both[pl.ds(0, count)] = refs.own[...]
        refs.both[pl.ds(count, count)] = refs.taken[...]

    outs = dict(both=VMEM((2 * count,) + own.shape[1:], own.dtype))
    return kernel_call("join", body, dict(own=In(own, VMEM), taken=In(taken, VMEM)), outs).both


def answer(z, info, cols, which, flips, table, b, after):
    outs = {"m" + str(flip): z.message() for flip in flips}

    def body(refs):
        gathers = [
            Gather(z, refs, getattr(refs, name), flip, which, refs.sems.at[flip]) for name, flip in zip(outs, flips)
        ]
        for gather in gathers:
            gather.start()
        for gather in gathers:
            gather.finish()

    return kernel_call(
        "answer",
        body,
        dict(
            info=In(info, SMEM),
            cols_s=In(cols, SMEM),
            cols_v=In(cols, VMEM),
            table=In(table, VMEM),
            b=In(b, HBM),
            after=In(after, ANY),
        ),
        outs,
        scratch=dict(sems=DMA((2,))),
    )


def own_blocks(z, info, cols, table, b, kept, after):
    def body(refs):
        answer = Gather(z, refs, refs.message, 1, 0, refs.sems.at[0])
        local = Gather(z, refs, refs.local, 0, 0, refs.sems.at[1])
        local.start()
        answer.start()
        clear(refs.acc)
        local.finish()
        add = Add(z, refs, [(refs.kept.at[0], refs.local)])
        add.start()
        answer.finish()
        add.finish()

    return kernel_call(
        "own_blocks",
        body,
        dict(
            info=In(info, SMEM),
            cols_s=In(cols, SMEM),
            cols_v=In(cols, VMEM),
            table=In(table, VMEM),
            b=In(b, HBM),
            kept=In(kept, VMEM),
            after=In(after, ANY),
        ),
        dict(acc=z.window(), message=z.message()),
        scratch=dict(sems=DMA((2,)), local=z.message(), **add_scratch(z)),
    )


def add_messages(z, info, left, arrived, acc, answer=None, after=None, write=False):
    ins = dict(info=In(info, SMEM), left=In(left, VMEM), acc_in=In(acc, VMEM))
    taken = {"m" + str(at): In(message, VMEM) for at, (_, _, message) in enumerate(arrived)}
    ins.update(taken)
    outs = dict(acc=z.window())
    aliases = [("acc_in", "acc")]
    scratch = add_scratch(z, len(arrived))
    if answer is not None:
        cols, which, side, table, b = answer
        ins.update(cols_s=In(cols, SMEM), cols_v=In(cols, VMEM), table=In(table, VMEM), b=In(b, HBM))
        outs.update(message=z.message())
        scratch.update(sems=DMA((1,)))
    if after is not None:
        ins.update(after=In(after, ANY))
    if write:
        outs.update(out=jax.ShapeDtypeStruct((z.half, z.bs, JW * z.bs), BF16))
        scratch.update(WriteAll.scratch(z))

    def body(refs):
        if answer is not None:
            gather = Gather(z, refs, refs.message, side, which, refs.sems.at[0])
            gather.start()
        pairs = []
        for name, (by, flip, _) in zip(taken, arrived):
            place = flip if by == 0 else refs.info[1 + by] * 2 + flip
            pairs.append((refs.left.at[place], getattr(refs, name)))
        add = Add(z, refs, pairs)
        add.start()
        if answer is not None:
            gather.finish()
        if write:
            writer = WriteAll(z, refs)
            add.finish(writer.row)
            writer.finish()
        else:
            add.finish()

    return kernel_call("add_messages", body, ins, outs, aliases, scratch)


def on_device(a_blocks, a_scale, a_cols, b_blocks, b_scale, b_cols):
    panels = lax.axis_size(ROW)
    columns = lax.axis_size(COL)
    halves = columns // panels
    a_part, a_scl, a_pos = a_blocks[0, 0], a_scale[0, 0].T, a_cols[0, 0].T
    b_part = b_blocks[0, 0]
    b_scl, b_pos = b_scale[0, 0].T, b_cols[0, 0].T
    nrows, bs, _ = a_part.shape
    z = Sizes(nrows // halves, a_scl.shape[0], b_scl.shape[0], bs)
    row = lax.axis_index(ROW)
    parity = lax.axis_index(COL) % halves
    info = jnp.stack([parity] + [row ^ ((row - by) % panels) for by in range(panels)]).astype(I32)

    def step(value, by, flip):
        pairs = [
            (c, ((c // halves + by) % panels) * halves + (c % halves ^ flip)) for c in range(columns)
        ]
        return lax.ppermute(value, COL, pairs)

    def named_by(by, cols):
        pairs = []
        for r in range(panels):
            for c in range(columns):
                to_row = (r + by) % panels
                to_col = (c - halves * by) % columns
                pairs.append((r * columns + c, to_row * columns + to_col))
        return lax.ppermute(cols, (ROW, COL), pairs)

    order = sorted(range(1, panels), key=lambda by: -min(by, panels - by))
    last = order[-1]
    own_cols = a_pos[None]

    first_cols = named_by(order[0], own_cols)
    ready = prepare(info, own_cols, b_scl, b_pos)
    own_cols, table = ready.own, ready.table
    cols = join(own_cols, first_cols)
    asked, known, by = {0: (own_cols, 0)}, [0, order[0]], panels // 4
    more_cols = named_by(by, cols)
    got = answer(z, info, cols, 1, (0, 1), table, b_part, table)
    after = got.m0
    moving = {(order[0], flip): step(one, order[0], flip) for flip, one in enumerate((got.m0, got.m1))}
    pieces = split(z, info, a_part.reshape(nrows * bs, z.wide), a_scl, after, more_cols)
    while True:
        asked.update({(to + by) % panels: (more_cols, at) for at, to in enumerate(known)})
        known += [(to + by) % panels for to in known]
        by //= 2
        if not by:
            break
        cols = join(cols, more_cols)
        more_cols = named_by(by, cols)

    own_left = join(pieces.kept, step(pieces.given, 0, 1))
    left = own_left
    bit = 1
    while bit < panels:
        left = join(left, lax.ppermute(left, ROW, [(r, r ^ bit) for r in range(panels)]))
        bit *= 2

    mine = own_blocks(z, info, own_cols, table, b_part, pieces.kept, after)
    taken = step(mine.message, 0, 1)
    after = mine.message
    for by in order[1:-1]:
        for flip in range(halves):
            got = answer(z, info, *asked[by], (flip,), table, b_part, after)
            (after,) = vars(got).values()
            moving[by, flip] = step(after, by, flip)

    got = add_messages(
        z, info, own_left, [(0, 1, taken)], mine.acc, (*asked[last], 0, table, b_part), after=after
    )
    acc, ends = got.acc, [got.message]
    early = [(by, flip) for by in order[:-1] for flip in range(halves)]
    for at, (by, flip) in enumerate(early[:-1]):
        got = add_messages(
            z, info, left, [(by, flip, moving[by, flip])], acc,
            (*asked[last], 1, table, b_part) if at == 0 else None, after=ends[0] if at == 0 else None,
        )
        acc = got.acc
        if at == 0:
            ends.append(got.message)
    final = [(*early[-1], moving[early[-1]])]
    final += [(last, flip, step(ends[flip], last, flip)) for flip in range(halves)]
    out = add_messages(z, info, left, final, acc, write=True).out
    return out[None, None]


def solution(mesh):
    in_specs = (
        P(COL, ROW, None, None, None),
        P(COL, ROW, None, None),
        P(COL, ROW, None, None),
        P(COL, ROW, None, None, None),
        P(COL, ROW, None, None),
        P(COL, ROW, None, None),
    )
    out_specs = P(COL, ROW, None, None, None)
    return jax.shard_map(
        on_device, mesh=mesh, in_specs=in_specs, out_specs=out_specs, check_vma=False
    )
```

```python
import types

import jax
import jax.numpy as jnp
from jax import lax
from jax.experimental import pallas as pl
from jax.experimental.pallas import tpu as pltpu
from jax.sharding import PartitionSpec as P

JW = 512
LANES = 128
META = 16
PARTS = 5
CHUNKS = 4
SLOTS = 8
ROW, COL = "row", "col"
F32, BF16, I32 = jnp.float32, jnp.bfloat16, jnp.int32
VMEM_LIMIT = 12 * 1024 * 1024
SMEM, VMEM, HBM, ANY = pltpu.SMEM, pltpu.VMEM, pltpu.HBM, pl.ANY
DMA = pltpu.SemaphoreType.DMA
copy = pltpu.make_async_copy


def three_parts(x):
    high = x.astype(BF16).astype(F32)
    rest = x - high
    mid = rest.astype(BF16).astype(F32)
    return [high, mid, (rest - mid).astype(BF16).astype(F32)]


def stacked(parts, rows):
    which = lax.broadcasted_iota(I32, (rows, parts[0].shape[1]), 0)
    tile = jnp.zeros(which.shape, F32)
    for at, part in enumerate(parts):
        tile = jnp.where(which == at, jnp.broadcast_to(part, which.shape), tile)
    return tile


def entries(values, first, half, rb):
    ra = values.shape[0]
    one = [values[m : m + 1, first : first + half] for m in range(ra)]
    return jnp.concatenate(one * rb, axis=1)


class Sizes:
    def __init__(self, half, ra, rb, bs):
        self.half, self.ra, self.rb, self.bs = half, ra, rb, bs
        self.wide = ra * bs
        self.tiles = JW * bs // LANES

    def message(self):
        return VMEM((self.half * self.wide + META, self.rb * self.bs), BF16)

    def window(self):
        return VMEM((self.half, self.tiles, self.bs, LANES), F32)


class In:
    def __init__(self, array, place):
        self.array, self.place = array, place
        if place in (VMEM, HBM):
            self.array = pltpu.with_memory_space_constraint(array, place)


def kernel_call(name, body, ins, outs, aliases=(), scratch=None):
    names = list(ins) + list(outs) + list(scratch or {})

    def kernel(*refs):
        body(types.SimpleNamespace(**dict(zip(names, refs))))

    def out_place(shape):
        return ANY if isinstance(shape, jax.ShapeDtypeStruct) else VMEM

    got = pl.pallas_call(
        kernel,
        out_shape=list(outs.values()),
        in_specs=[pl.BlockSpec(memory_space=one.place) for one in ins.values()],
        out_specs=[pl.BlockSpec(memory_space=out_place(shape)) for shape in outs.values()],
        input_output_aliases={list(ins).index(a): list(outs).index(b) for a, b in aliases},
        scratch_shapes=list((scratch or {}).values()),
        compiler_params=pltpu.CompilerParams(vmem_limit_bytes=VMEM_LIMIT),
        cost_estimate=pl.CostEstimate(flops=2 * 10**10, bytes_accessed=1024, transcendentals=0),
        name=name,
    )(*[one.array for one in ins.values()])
    return types.SimpleNamespace(**dict(zip(outs, got)))


class Gather:
    def __init__(self, z, refs, message, flip, which, sem):
        self.z, self.refs, self.message, self.flip, self.which, self.sem = z, refs, message, flip, which, sem

    def start(self):
        z, refs = self.z, self.refs
        cols = refs.cols_s.at[self.which]
        base = (refs.info[0] ^ self.flip) * z.half

        def one_row(i, _):
            for m in range(z.ra):
                at = pl.multiple_of((i * z.ra + m) * z.bs, z.bs)
                copy(refs.b.at[cols[m, base + i]], self.message.at[pl.ds(at, z.bs)], self.sem).start()
            return 0

        lax.fori_loop(0, z.half, one_row, 0, unroll=2)

    def finish(self):
        z, refs = self.z, self.refs
        table, cols = refs.table, refs.cols_v[self.which]
        kw = table.shape[1]
        both = [entries(cols, h * z.half, z.half, z.rb) for h in range(2)]
        named = jnp.where((refs.info[0] ^ self.flip) == 1, both[1], both[0])
        named = jnp.broadcast_to(named, (kw, named.shape[1]))
        picked = lax.broadcasted_iota(I32, named.shape, 0) == named
        picked = jnp.where(picked, 1.0, 0.0).astype(BF16)
        found = jnp.dot(table[...], picked, preferred_element_type=F32)
        slot = lax.broadcasted_iota(I32, (1, found.shape[1]), 1) // (z.ra * z.half)
        parts = []
        for part in range(PARTS):
            value = found[part * z.rb : part * z.rb + 1]
            for n in range(1, z.rb):
                value = jnp.where(slot == n, found[part * z.rb + n : part * z.rb + n + 1], value)
            parts.append(value)
        size = z.half * z.wide
        self.message[pl.ds(size, META), :] = stacked(parts, META).astype(BF16)
        blocks = self.message.at[pl.ds(0, size)]
        copy(blocks, blocks, self.sem).wait()


def add_scratch(z, count=1):
    return dict(
        prods=VMEM((count, z.half * z.wide, LANES), F32),
        scl_v=VMEM((8, LANES), F32),
        col_v=VMEM((8, LANES), I32),
        scl_s=SMEM((8, LANES), F32),
        col_s=SMEM((8, LANES), I32),
        add_sems=DMA((2,)),
    )


class Add:
    def __init__(self, z, refs, pairs):
        self.z, self.refs, self.pairs = z, refs, pairs

    def start(self):
        z, refs = self.z, self.refs
        for at, (a, b) in enumerate(self.pairs):
            a_meta = a[pl.ds(a.shape[0] - META, META), :].astype(F32)
            b_meta = b[pl.ds(b.shape[0] - META, META), :].astype(F32)
            scl_a = a_meta[0:1] + a_meta[1:2] + a_meta[2:3]
            scl_b = b_meta[0:1] + b_meta[1:2] + b_meta[2:3]
            refs.scl_v[at : at + 1, :] = scl_a * scl_b
            refs.col_v[at : at + 1, :] = (b_meta[3:4] * 256.0 + b_meta[4:5]).astype(I32)
        self.moves = [
            copy(refs.scl_v, refs.scl_s, refs.add_sems.at[0]),
            copy(refs.col_v, refs.col_s, refs.add_sems.at[1]),
        ]
        for move in self.moves:
            move.start()
        row_block = lax.broadcasted_iota(I32, (z.wide, z.wide), 0) // z.bs
        col_block = lax.broadcasted_iota(I32, (z.wide, z.wide), 1) // z.bs
        diagonal = jnp.where(row_block == col_block, 1.0, 0.0).astype(BF16)
        for at, (a, b) in enumerate(self.pairs):
            for i in range(z.half):
                left = a[pl.ds(i * z.bs, z.bs), :]
                left = jnp.concatenate([left] * z.ra, axis=0) * diagonal
                rows = pl.ds(i * z.wide, z.wide)
                refs.prods[at, rows, :] = jnp.dot(left, b[rows, :], preferred_element_type=F32)

    def finish(self, after_row=None):
        z, refs, acc = self.z, self.refs, self.refs.acc
        per = LANES // z.bs
        for move in self.moves:
            move.wait()
        lane_block = lax.broadcasted_iota(I32, (8, LANES), 1) // z.bs
        for i in range(z.half):
            for at in range(len(self.pairs)):
                for m in range(z.ra):
                    value = refs.prods[at, pl.ds((i * z.ra + m) * z.bs, z.bs), :]
                    placed = []
                    for n in range(z.rb):
                        entry = (n * z.ra + m) * z.half + i
                        column = refs.col_s[at, entry]
                        place = column & (per - 1)
                        moved = pltpu.roll(value, ((place - n) & (per - 1)) * z.bs, 1)
                        scale = jnp.where(lane_block == place, refs.scl_s[at, entry], 0.0)
                        placed.append((column // per, moved * jnp.concatenate([scale] * (z.bs // 8), axis=0)))
                    for tile, moved in placed:
                        acc[i, tile] = acc[i, tile] + moved
            if after_row is not None:
                after_row(i)


def clear(acc):
    for i in range(acc.shape[0]):

        def clear_tile(tile, _, i=i):
            acc[i, tile] = jnp.zeros(acc.shape[2:], F32)
            return 0

        lax.fori_loop(0, acc.shape[1], clear_tile, 0, unroll=8)


class WriteAll:
    def __init__(self, z, refs):
        self.z, self.refs, self.sent = z, refs, []

    @staticmethod
    def scratch(z):
        return dict(stage=VMEM((SLOTS, z.bs, JW * z.bs // CHUNKS), BF16), out_sems=DMA((SLOTS,)))

    def send(self, at):
        i, chunk = self.sent[at]
        slot, width = at % SLOTS, self.refs.stage.shape[2]
        there = self.refs.out.at[i, :, pl.ds(chunk * width, width)]
        return copy(self.refs.stage.at[slot], there, self.refs.out_sems.at[slot])

    def row(self, i):
        acc, stage = self.refs.acc, self.refs.stage
        tiles = self.z.tiles // CHUNKS
        for chunk in range(CHUNKS):
            at = len(self.sent)
            if at >= SLOTS:
                self.send(at - SLOTS).wait()
            for tile in range(tiles):
                piece = acc[i, chunk * tiles + tile].astype(BF16)
                stage[at % SLOTS, :, pl.ds(tile * LANES, LANES)] = piece
            self.sent.append((i, chunk))
            self.send(at).start()

    def finish(self):
        for at in range(max(0, len(self.sent) - SLOTS), len(self.sent)):
            self.send(at).wait()


def prepare(info, own_cols, b_scl, b_pos):
    rb, kw = b_scl.shape

    def body(refs):
        moves = [
            copy(refs.b_scl, refs.scl, refs.sems.at[0]),
            copy(refs.b_pos, refs.pos, refs.sems.at[1]),
            copy(refs.own_cols, refs.own, refs.sems.at[2]),
        ]
        for move in moves:
            move.start()
        for move in moves:
            move.wait()
        scale, column = refs.scl[...], refs.pos[...]
        table = three_parts(scale) + [(column >> 8).astype(F32), (column & 255).astype(F32)]
        table.append(jnp.zeros((refs.table.shape[0] - PARTS * rb, kw), F32))
        refs.table[...] = jnp.concatenate(table, axis=0).astype(BF16)

    return kernel_call(
        "prepare",
        body,
        dict(info=In(info, SMEM), own_cols=In(own_cols, HBM), b_scl=In(b_scl, HBM), b_pos=In(b_pos, HBM)),
        dict(table=VMEM((-(-PARTS * rb // 16) * 16, kw), BF16), own=VMEM(own_cols.shape, I32)),
        scratch=dict(scl=VMEM(b_scl.shape, F32), pos=VMEM(b_pos.shape, I32), sems=DMA((3,))),
    )


def split(z, info, a, a_scl, after, asked):
    def body(refs):
        scale = refs.a_scl[...]
        both = [entries(scale, h * z.half, z.half, z.rb) for h in range(2)]
        size = z.half * z.bs
        for flip, out in enumerate((refs.kept, refs.given)):
            side = refs.info[0] ^ flip
            out[0, pl.ds(0, size), :] = refs.a[pl.ds(pl.multiple_of(side * size, size), size), :]
            parts = three_parts(jnp.where(side == 1, both[1], both[0]))
            out[0, pl.ds(size, META), :] = stacked(parts, META).astype(BF16)

    piece = VMEM((1, z.half * z.bs + META, z.wide), BF16)
    return kernel_call(
        "split",
        body,
        dict(
            info=In(info, SMEM), a=In(a, VMEM), a_scl=In(a_scl, VMEM), after=In(after, ANY), asked=In(asked, ANY)
        ),
        dict(kept=piece, given=piece),
    )


def join(own, taken):
    count = own.shape[0]

    def body(refs):
        refs.both[pl.ds(0, count)] = refs.own[...]
        refs.both[pl.ds(count, count)] = refs.taken[...]

    outs = dict(both=VMEM((2 * count,) + own.shape[1:], own.dtype))
    return kernel_call("join", body, dict(own=In(own, VMEM), taken=In(taken, VMEM)), outs).both


def answer(z, info, cols, which, flips, table, b, after):
    outs = {"m" + str(flip): z.message() for flip in flips}

    def body(refs):
        gathers = [
            Gather(z, refs, getattr(refs, name), flip, which, refs.sems.at[flip]) for name, flip in zip(outs, flips)
        ]
        for gather in gathers:
            gather.start()
        for gather in gathers:
            gather.finish()

    return kernel_call(
        "answer",
        body,
        dict(
            info=In(info, SMEM),
            cols_s=In(cols, SMEM),
            cols_v=In(cols, VMEM),
            table=In(table, VMEM),
            b=In(b, HBM),
            after=In(after, ANY),
        ),
        outs,
        scratch=dict(sems=DMA((2,))),
    )


def own_blocks(z, info, cols, table, b, kept, after):
    def body(refs):
        answer = Gather(z, refs, refs.message, 1, 0, refs.sems.at[0])
        local = Gather(z, refs, refs.local, 0, 0, refs.sems.at[1])
        local.start()
        answer.start()
        clear(refs.acc)
        local.finish()
        add = Add(z, refs, [(refs.kept.at[0], refs.local)])
        add.start()
        answer.finish()
        add.finish()

    return kernel_call(
        "own_blocks",
        body,
        dict(
            info=In(info, SMEM),
            cols_s=In(cols, SMEM),
            cols_v=In(cols, VMEM),
            table=In(table, VMEM),
            b=In(b, HBM),
            kept=In(kept, VMEM),
            after=In(after, ANY),
        ),
        dict(acc=z.window(), message=z.message()),
        scratch=dict(sems=DMA((2,)), local=z.message(), **add_scratch(z)),
    )


def add_messages(z, info, left, arrived, acc, answer=None, after=None, write=False):
    ins = dict(info=In(info, SMEM), left=In(left, VMEM), acc_in=In(acc, VMEM))
    taken = {"m" + str(at): In(message, VMEM) for at, (_, _, message) in enumerate(arrived)}
    ins.update(taken)
    outs = dict(acc=z.window())
    aliases = [("acc_in", "acc")]
    scratch = add_scratch(z, len(arrived))
    if answer is not None:
        cols, which, side, table, b = answer
        ins.update(cols_s=In(cols, SMEM), cols_v=In(cols, VMEM), table=In(table, VMEM), b=In(b, HBM))
        outs.update(message=z.message())
        scratch.update(sems=DMA((1,)))
    if after is not None:
        ins.update(after=In(after, ANY))
    if write:
        outs.update(out=jax.ShapeDtypeStruct((z.half, z.bs, JW * z.bs), BF16))
        scratch.update(WriteAll.scratch(z))

    def body(refs):
        if answer is not None:
            gather = Gather(z, refs, refs.message, side, which, refs.sems.at[0])
            gather.start()
        pairs = []
        for name, (by, flip, _) in zip(taken, arrived):
            place = flip if by == 0 else refs.info[1 + by] * 2 + flip
            pairs.append((refs.left.at[place], getattr(refs, name)))
        add = Add(z, refs, pairs)
        add.start()
        if answer is not None:
            gather.finish()
        if write:
            writer = WriteAll(z, refs)
            add.finish(writer.row)
            writer.finish()
        else:
            add.finish()

    return kernel_call("add_messages", body, ins, outs, aliases, scratch)


def on_device(a_blocks, a_scale, a_cols, b_blocks, b_scale, b_cols):
    panels = lax.axis_size(ROW)
    columns = lax.axis_size(COL)
    halves = columns // panels
    a_part, a_scl, a_pos = a_blocks[0, 0], a_scale[0, 0].T, a_cols[0, 0].T
    b_part = b_blocks[0, 0]
    b_scl, b_pos = b_scale[0, 0].T, b_cols[0, 0].T
    nrows, bs, _ = a_part.shape
    z = Sizes(nrows // halves, a_scl.shape[0], b_scl.shape[0], bs)
    row = lax.axis_index(ROW)
    parity = lax.axis_index(COL) % halves
    info = jnp.stack([parity] + [row ^ ((row - by) % panels) for by in range(panels)]).astype(I32)

    def step(value, by, flip):
        pairs = [
            (c, ((c // halves + by) % panels) * halves + (c % halves ^ flip)) for c in range(columns)
        ]
        return lax.ppermute(value, COL, pairs)

    def named_by(by, cols):
        pairs = []
        for r in range(panels):
            for c in range(columns):
                to_row = (r + by) % panels
                to_col = (c - halves * by) % columns
                pairs.append((r * columns + c, to_row * columns + to_col))
        return lax.ppermute(cols, (ROW, COL), pairs)

    order = sorted(range(1, panels), key=lambda by: -min(by, panels - by))
    last = order[-1]
    own_cols = a_pos[None]

    first_cols = named_by(order[0], own_cols)
    ready = prepare(info, own_cols, b_scl, b_pos)
    own_cols, table = ready.own, ready.table
    cols = join(own_cols, first_cols)
    asked, known, by = {0: (own_cols, 0)}, [0, order[0]], panels // 4
    more_cols = named_by(by, cols)
    got = answer(z, info, cols, 1, (0, 1), table, b_part, table)
    after = got.m0
    moving = {(order[0], flip): step(one, order[0], flip) for flip, one in enumerate((got.m0, got.m1))}
    pieces = split(z, info, a_part.reshape(nrows * bs, z.wide), a_scl, after, more_cols)
    while True:
        asked.update({(to + by) % panels: (more_cols, at) for at, to in enumerate(known)})
        known += [(to + by) % panels for to in known]
        by //= 2
        if not by:
            break
        cols = join(cols, more_cols)
        more_cols = named_by(by, cols)

    own_left = join(pieces.kept, step(pieces.given, 0, 1))
    left = own_left
    bit = 1
    while bit < panels:
        left = join(left, lax.ppermute(left, ROW, [(r, r ^ bit) for r in range(panels)]))
        bit *= 2

    mine = own_blocks(z, info, own_cols, table, b_part, pieces.kept, after)
    taken = step(mine.message, 0, 1)
    after = mine.message
    for by in order[1:-1]:
        for flip in range(halves):
            got = answer(z, info, *asked[by], (flip,), table, b_part, after)
            (after,) = vars(got).values()
            moving[by, flip] = step(after, by, flip)

    got = add_messages(
        z, info, own_left, [(0, 1, taken)], mine.acc, (*asked[last], 0, table, b_part), after=after
    )
    acc, ends = got.acc, [got.message]
    early = [(by, flip) for by in order[:-1] for flip in range(halves)]
    early[:halves] = early[halves - 1 :: -1]
    for at, (by, flip) in enumerate(early[:-1]):
        got = add_messages(
            z, info, left, [(by, flip, moving[by, flip])], acc,
            (*asked[last], 1, table, b_part) if at == 0 else None, after=ends[0] if at == 0 else None,
        )
        acc = got.acc
        if at == 0:
            ends.append(got.message)
    final = [(*early[-1], moving[early[-1]])]
    final += [(last, flip, step(ends[flip], last, flip)) for flip in range(halves)]
    out = add_messages(z, info, left, final, acc, write=True).out
    return out[None, None]


def solution(mesh):
    in_specs = (
        P(COL, ROW, None, None, None),
        P(COL, ROW, None, None),
        P(COL, ROW, None, None),
        P(COL, ROW, None, None, None),
        P(COL, ROW, None, None),
        P(COL, ROW, None, None),
    )
    out_specs = P(COL, ROW, None, None, None)
    return jax.shard_map(
        on_device, mesh=mesh, in_specs=in_specs, out_specs=out_specs, check_vma=False
    )
```

```python
import types

import jax
import jax.numpy as jnp
from jax import lax
from jax.experimental import pallas as pl
from jax.experimental.pallas import tpu as pltpu
from jax.sharding import PartitionSpec as P

JW = 512
LANES = 128
META = 16
PARTS = 5
CHUNKS = 4
SLOTS = 8
ROW, COL = "row", "col"
F32, BF16, I32 = jnp.float32, jnp.bfloat16, jnp.int32
VMEM_LIMIT = 12 * 1024 * 1024
SMEM, VMEM, HBM, ANY = pltpu.SMEM, pltpu.VMEM, pltpu.HBM, pl.ANY
DMA = pltpu.SemaphoreType.DMA
copy = pltpu.make_async_copy


def three_parts(x):
    high = x.astype(BF16).astype(F32)
    rest = x - high
    mid = rest.astype(BF16).astype(F32)
    return [high, mid, (rest - mid).astype(BF16).astype(F32)]


def stacked(parts, rows):
    which = lax.broadcasted_iota(I32, (rows, parts[0].shape[1]), 0)
    tile = jnp.zeros(which.shape, F32)
    for at, part in enumerate(parts):
        tile = jnp.where(which == at, jnp.broadcast_to(part, which.shape), tile)
    return tile


def entries(values, first, half, rb):
    ra = values.shape[0]
    one = [values[m : m + 1, first : first + half] for m in range(ra)]
    return jnp.concatenate(one * rb, axis=1)


class Sizes:
    def __init__(self, half, ra, rb, bs):
        self.half, self.ra, self.rb, self.bs = half, ra, rb, bs
        self.wide = ra * bs
        self.tiles = JW * bs // LANES

    def message(self):
        return VMEM((self.half * self.wide + META, self.rb * self.bs), BF16)

    def window(self):
        return VMEM((self.half, self.tiles, self.bs, LANES), F32)


class In:
    def __init__(self, array, place):
        self.array, self.place = array, place
        if place in (VMEM, HBM):
            self.array = pltpu.with_memory_space_constraint(array, place)


def kernel_call(name, body, ins, outs, aliases=(), scratch=None):
    names = list(ins) + list(outs) + list(scratch or {})

    def kernel(*refs):
        body(types.SimpleNamespace(**dict(zip(names, refs))))

    def out_place(shape):
        return ANY if isinstance(shape, jax.ShapeDtypeStruct) else VMEM

    got = pl.pallas_call(
        kernel,
        out_shape=list(outs.values()),
        in_specs=[pl.BlockSpec(memory_space=one.place) for one in ins.values()],
        out_specs=[pl.BlockSpec(memory_space=out_place(shape)) for shape in outs.values()],
        input_output_aliases={list(ins).index(a): list(outs).index(b) for a, b in aliases},
        scratch_shapes=list((scratch or {}).values()),
        compiler_params=pltpu.CompilerParams(vmem_limit_bytes=VMEM_LIMIT),
        cost_estimate=pl.CostEstimate(flops=2 * 10**10, bytes_accessed=1024, transcendentals=0),
        name=name,
    )(*[one.array for one in ins.values()])
    return types.SimpleNamespace(**dict(zip(outs, got)))


class Gather:
    def __init__(self, z, refs, message, flip, which, sem):
        self.z, self.refs, self.message, self.flip, self.which, self.sem = z, refs, message, flip, which, sem

    def start(self):
        z, refs = self.z, self.refs
        cols = refs.cols_s.at[self.which]
        base = (refs.info[0] ^ self.flip) * z.half

        def one_row(i, _):
            for m in range(z.ra):
                at = pl.multiple_of((i * z.ra + m) * z.bs, z.bs)
                copy(refs.b.at[cols[m, base + i]], self.message.at[pl.ds(at, z.bs)], self.sem).start()
            return 0

        lax.fori_loop(0, z.half, one_row, 0, unroll=2)

    def finish(self):
        z, refs = self.z, self.refs
        table, cols = refs.table, refs.cols_v[self.which]
        kw = table.shape[1]
        both = [entries(cols, h * z.half, z.half, z.rb) for h in range(2)]
        named = jnp.where((refs.info[0] ^ self.flip) == 1, both[1], both[0])
        named = jnp.broadcast_to(named, (kw, named.shape[1]))
        picked = lax.broadcasted_iota(I32, named.shape, 0) == named
        picked = jnp.where(picked, 1.0, 0.0).astype(BF16)
        found = jnp.dot(table[...], picked, preferred_element_type=F32)
        slot = lax.broadcasted_iota(I32, (1, found.shape[1]), 1) // (z.ra * z.half)
        parts = []
        for part in range(PARTS):
            value = found[part * z.rb : part * z.rb + 1]
            for n in range(1, z.rb):
                value = jnp.where(slot == n, found[part * z.rb + n : part * z.rb + n + 1], value)
            parts.append(value)
        size = z.half * z.wide
        self.message[pl.ds(size, META), :] = stacked(parts, META).astype(BF16)
        blocks = self.message.at[pl.ds(0, size)]
        copy(blocks, blocks, self.sem).wait()


def add_scratch(z, count=1):
    return dict(
        prods=VMEM((count, z.half * z.wide, LANES), F32),
        scl_v=VMEM((8, LANES), F32),
        col_v=VMEM((8, LANES), I32),
        scl_s=SMEM((8, LANES), F32),
        col_s=SMEM((8, LANES), I32),
        add_sems=DMA((2,)),
    )


class Add:
    def __init__(self, z, refs, pairs):
        self.z, self.refs, self.pairs = z, refs, pairs

    def start(self):
        z, refs = self.z, self.refs
        for at, (a, b) in enumerate(self.pairs):
            a_meta = a[pl.ds(a.shape[0] - META, META), :].astype(F32)
            b_meta = b[pl.ds(b.shape[0] - META, META), :].astype(F32)
            scl_a = a_meta[0:1] + a_meta[1:2] + a_meta[2:3]
            scl_b = b_meta[0:1] + b_meta[1:2] + b_meta[2:3]
            refs.scl_v[at : at + 1, :] = scl_a * scl_b
            refs.col_v[at : at + 1, :] = (b_meta[3:4] * 256.0 + b_meta[4:5]).astype(I32)
        self.moves = [
            copy(refs.scl_v, refs.scl_s, refs.add_sems.at[0]),
            copy(refs.col_v, refs.col_s, refs.add_sems.at[1]),
        ]
        for move in self.moves:
            move.start()
        row_block = lax.broadcasted_iota(I32, (z.wide, z.wide), 0) // z.bs
        col_block = lax.broadcasted_iota(I32, (z.wide, z.wide), 1) // z.bs
        diagonal = jnp.where(row_block == col_block, 1.0, 0.0).astype(BF16)
        for at, (a, b) in enumerate(self.pairs):
            for i in range(z.half):
                left = a[pl.ds(i * z.bs, z.bs), :]
                left = jnp.concatenate([left] * z.ra, axis=0) * diagonal
                rows = pl.ds(i * z.wide, z.wide)
                refs.prods[at, rows, :] = jnp.dot(left, b[rows, :], preferred_element_type=F32)

    def finish(self, after_row=None):
        z, refs, acc = self.z, self.refs, self.refs.acc
        per = LANES // z.bs
        for move in self.moves:
            move.wait()
        lane_block = lax.broadcasted_iota(I32, (8, LANES), 1) // z.bs
        for i in range(z.half):
            for at in range(len(self.pairs)):
                for m in range(z.ra):
                    value = refs.prods[at, pl.ds((i * z.ra + m) * z.bs, z.bs), :]
                    placed = []
                    for n in range(z.rb):
                        entry = (n * z.ra + m) * z.half + i
                        column = refs.col_s[at, entry]
                        place = column & (per - 1)
                        moved = pltpu.roll(value, ((place - n) & (per - 1)) * z.bs, 1)
                        scale = jnp.where(lane_block == place, refs.scl_s[at, entry], 0.0)
                        placed.append((column // per, moved * jnp.concatenate([scale] * (z.bs // 8), axis=0)))
                    for tile, moved in placed:
                        acc[i, tile] = acc[i, tile] + moved
            if after_row is not None:
                after_row(i)


def clear(acc):
    for i in range(acc.shape[0]):

        def clear_tile(tile, _, i=i):
            acc[i, tile] = jnp.zeros(acc.shape[2:], F32)
            return 0

        lax.fori_loop(0, acc.shape[1], clear_tile, 0, unroll=8)


class WriteAll:
    def __init__(self, z, refs):
        self.z, self.refs, self.sent = z, refs, []

    @staticmethod
    def scratch(z):
        return dict(stage=VMEM((SLOTS, z.bs, JW * z.bs // CHUNKS), BF16), out_sems=DMA((SLOTS,)))

    def send(self, at):
        i, chunk = self.sent[at]
        slot, width = at % SLOTS, self.refs.stage.shape[2]
        there = self.refs.out.at[i, :, pl.ds(chunk * width, width)]
        return copy(self.refs.stage.at[slot], there, self.refs.out_sems.at[slot])

    def row(self, i):
        acc, stage = self.refs.acc, self.refs.stage
        tiles = self.z.tiles // CHUNKS
        for chunk in range(CHUNKS):
            at = len(self.sent)
            if at >= SLOTS:
                self.send(at - SLOTS).wait()
            for tile in range(tiles):
                piece = acc[i, chunk * tiles + tile].astype(BF16)
                stage[at % SLOTS, :, pl.ds(tile * LANES, LANES)] = piece
            self.sent.append((i, chunk))
            self.send(at).start()

    def finish(self):
        for at in range(max(0, len(self.sent) - SLOTS), len(self.sent)):
            self.send(at).wait()


def prepare(info, own_cols, b_scl, b_pos):
    rb, kw = b_scl.shape

    def body(refs):
        moves = [
            copy(refs.b_scl, refs.scl, refs.sems.at[0]),
            copy(refs.b_pos, refs.pos, refs.sems.at[1]),
            copy(refs.own_cols, refs.own, refs.sems.at[2]),
        ]
        for move in moves:
            move.start()
        for move in moves:
            move.wait()
        scale, column = refs.scl[...], refs.pos[...]
        table = three_parts(scale) + [(column >> 8).astype(F32), (column & 255).astype(F32)]
        table.append(jnp.zeros((refs.table.shape[0] - PARTS * rb, kw), F32))
        refs.table[...] = jnp.concatenate(table, axis=0).astype(BF16)

    return kernel_call(
        "prepare",
        body,
        dict(info=In(info, SMEM), own_cols=In(own_cols, HBM), b_scl=In(b_scl, HBM), b_pos=In(b_pos, HBM)),
        dict(table=VMEM((-(-PARTS * rb // 16) * 16, kw), BF16), own=VMEM(own_cols.shape, I32)),
        scratch=dict(scl=VMEM(b_scl.shape, F32), pos=VMEM(b_pos.shape, I32), sems=DMA((3,))),
    )


def split(z, info, a, a_scl, after, asked):
    def body(refs):
        scale = refs.a_scl[...]
        both = [entries(scale, h * z.half, z.half, z.rb) for h in range(2)]
        size = z.half * z.bs
        for flip, out in enumerate((refs.kept, refs.given)):
            side = refs.info[0] ^ flip
            out[0, pl.ds(0, size), :] = refs.a[pl.ds(pl.multiple_of(side * size, size), size), :]
            parts = three_parts(jnp.where(side == 1, both[1], both[0]))
            out[0, pl.ds(size, META), :] = stacked(parts, META).astype(BF16)

    piece = VMEM((1, z.half * z.bs + META, z.wide), BF16)
    return kernel_call(
        "split",
        body,
        dict(
            info=In(info, SMEM), a=In(a, VMEM), a_scl=In(a_scl, VMEM), after=In(after, ANY), asked=In(asked, ANY)
        ),
        dict(kept=piece, given=piece),
    )


def join(own, taken):
    count = own.shape[0]

    def body(refs):
        refs.both[pl.ds(0, count)] = refs.own[...]
        refs.both[pl.ds(count, count)] = refs.taken[...]

    outs = dict(both=VMEM((2 * count,) + own.shape[1:], own.dtype))
    return kernel_call("join", body, dict(own=In(own, VMEM), taken=In(taken, VMEM)), outs).both


def answer(z, info, cols, which, flips, table, b, after):
    outs = {"m" + str(flip): z.message() for flip in flips}

    def body(refs):
        gathers = [
            Gather(z, refs, getattr(refs, name), flip, which, refs.sems.at[flip]) for name, flip in zip(outs, flips)
        ]
        for gather in gathers:
            gather.start()
        for gather in gathers:
            gather.finish()

    return kernel_call(
        "answer",
        body,
        dict(
            info=In(info, SMEM),
            cols_s=In(cols, SMEM),
            cols_v=In(cols, VMEM),
            table=In(table, VMEM),
            b=In(b, HBM),
            after=In(after, ANY),
        ),
        outs,
        scratch=dict(sems=DMA((2,))),
    )


def own_blocks(z, info, cols, table, b, kept, after):
    def body(refs):
        answer = Gather(z, refs, refs.message, 1, 0, refs.sems.at[0])
        local = Gather(z, refs, refs.local, 0, 0, refs.sems.at[1])
        local.start()
        answer.start()
        clear(refs.acc)
        local.finish()
        add = Add(z, refs, [(refs.kept.at[0], refs.local)])
        add.start()
        answer.finish()
        add.finish()

    return kernel_call(
        "own_blocks",
        body,
        dict(
            info=In(info, SMEM),
            cols_s=In(cols, SMEM),
            cols_v=In(cols, VMEM),
            table=In(table, VMEM),
            b=In(b, HBM),
            kept=In(kept, VMEM),
            after=In(after, ANY),
        ),
        dict(acc=z.window(), message=z.message()),
        scratch=dict(sems=DMA((2,)), local=z.message(), **add_scratch(z)),
    )


def add_messages(z, info, left, arrived, acc, answer=None, after=None, write=False):
    ins = dict(info=In(info, SMEM), left=In(left, VMEM), acc_in=In(acc, VMEM))
    taken = {"m" + str(at): In(message, VMEM) for at, (_, _, message) in enumerate(arrived)}
    ins.update(taken)
    outs = dict(acc=z.window())
    aliases = [("acc_in", "acc")]
    scratch = add_scratch(z, len(arrived))
    if answer is not None:
        cols, which, side, table, b = answer
        ins.update(cols_s=In(cols, SMEM), cols_v=In(cols, VMEM), table=In(table, VMEM), b=In(b, HBM))
        outs.update(message=z.message())
        scratch.update(sems=DMA((1,)))
    if after is not None:
        ins.update(after=In(after, ANY))
    if write:
        outs.update(out=jax.ShapeDtypeStruct((z.half, z.bs, JW * z.bs), BF16))
        scratch.update(WriteAll.scratch(z))

    def body(refs):
        if answer is not None:
            gather = Gather(z, refs, refs.message, side, which, refs.sems.at[0])
            gather.start()
        pairs = []
        for name, (by, flip, _) in zip(taken, arrived):
            place = flip if by == 0 else refs.info[1 + by] * 2 + flip
            pairs.append((refs.left.at[place], getattr(refs, name)))
        add = Add(z, refs, pairs)
        add.start()
        if answer is not None:
            gather.finish()
        if write:
            writer = WriteAll(z, refs)
            add.finish(writer.row)
            writer.finish()
        else:
            add.finish()

    return kernel_call("add_messages", body, ins, outs, aliases, scratch)


def on_device(a_blocks, a_scale, a_cols, b_blocks, b_scale, b_cols):
    panels = lax.axis_size(ROW)
    columns = lax.axis_size(COL)
    halves = columns // panels
    a_part, a_scl, a_pos = a_blocks[0, 0], a_scale[0, 0].T, a_cols[0, 0].T
    b_part = b_blocks[0, 0]
    b_scl, b_pos = b_scale[0, 0].T, b_cols[0, 0].T
    nrows, bs, _ = a_part.shape
    z = Sizes(nrows // halves, a_scl.shape[0], b_scl.shape[0], bs)
    row = lax.axis_index(ROW)
    parity = lax.axis_index(COL) % halves
    info = jnp.stack([parity] + [row ^ ((row - by) % panels) for by in range(panels)]).astype(I32)

    def step(value, by, flip):
        pairs = [
            (c, ((c // halves + by) % panels) * halves + (c % halves ^ flip)) for c in range(columns)
        ]
        return lax.ppermute(value, COL, pairs)

    def named_by(by, cols):
        pairs = []
        for r in range(panels):
            for c in range(columns):
                to_row = (r + by) % panels
                to_col = (c - halves * by) % columns
                pairs.append((r * columns + c, to_row * columns + to_col))
        return lax.ppermute(cols, (ROW, COL), pairs)

    order = sorted(range(1, panels), key=lambda by: -min(by, panels - by))
    last = order[-1]
    own_cols = a_pos[None]

    first_cols = named_by(order[0], own_cols)
    ready = prepare(info, own_cols, b_scl, b_pos)
    own_cols, table = ready.own, ready.table
    cols = join(own_cols, first_cols)
    asked, known, by = {0: (own_cols, 0)}, [0, order[0]], panels // 4
    more_cols = named_by(by, cols)
    got = answer(z, info, cols, 1, (0, 1), table, b_part, table)
    after = got.m0
    moving = {(order[0], flip): step(one, order[0], flip) for flip, one in enumerate((got.m0, got.m1))}
    pieces = split(z, info, a_part.reshape(nrows * bs, z.wide), a_scl, after, more_cols)
    while True:
        asked.update({(to + by) % panels: (more_cols, at) for at, to in enumerate(known)})
        known += [(to + by) % panels for to in known]
        by //= 2
        if not by:
            break
        cols = join(cols, more_cols)
        more_cols = named_by(by, cols)

    own_left = join(pieces.kept, step(pieces.given, 0, 1))
    left = own_left
    bit = 1
    while bit < panels:
        left = join(left, lax.ppermute(left, ROW, [(r, r ^ bit) for r in range(panels)]))
        bit *= 2

    mine = own_blocks(z, info, own_cols, table, b_part, pieces.kept, after)
    taken = step(mine.message, 0, 1)
    after = mine.message
    for by in order[1:-1]:
        for flip in range(halves):
            got = answer(z, info, *asked[by], (flip,), table, b_part, after)
            (after,) = vars(got).values()
            moving[by, flip] = step(after, by, flip)

    got = add_messages(
        z, info, own_left, [(0, 1, taken)], mine.acc, (*asked[last], 0, table, b_part), after=after
    )
    acc, ends = got.acc, [got.message]
    ends.append(answer(z, info, *asked[last], (1,), table, b_part, ends[0]).m1)
    early = [(by, flip) for by in order[:-1] for flip in range(halves)]
    early[:halves] = early[halves - 1 :: -1]
    after = ends[1]
    for by, flip in early[:-1]:
        acc = add_messages(z, info, left, [(by, flip, moving[by, flip])], acc, after=after).acc
        after = None
    both = [(*early[-1], moving[early[-1]]), (last, 0, step(ends[0], last, 0))]
    acc = add_messages(z, info, left, both, acc).acc
    out = add_messages(z, info, left, [(last, 1, step(ends[1], last, 1))], acc, write=True).out
    return out[None, None]


def solution(mesh):
    in_specs = (
        P(COL, ROW, None, None, None),
        P(COL, ROW, None, None),
        P(COL, ROW, None, None),
        P(COL, ROW, None, None, None),
        P(COL, ROW, None, None),
        P(COL, ROW, None, None),
    )
    out_specs = P(COL, ROW, None, None, None)
    return jax.shard_map(
        on_device, mesh=mesh, in_specs=in_specs, out_specs=out_specs, check_vma=False
    )
```

```python
import types

import jax
import jax.numpy as jnp
from jax import lax
from jax.experimental import pallas as pl
from jax.experimental.pallas import tpu as pltpu
from jax.sharding import PartitionSpec as P

JW = 512
LANES = 128
META = 16
PARTS = 5
CHUNKS = 4
SLOTS = 8
ROW, COL = "row", "col"
F32, BF16, I32 = jnp.float32, jnp.bfloat16, jnp.int32
VMEM_LIMIT = 12 * 1024 * 1024
SMEM, VMEM, HBM, ANY = pltpu.SMEM, pltpu.VMEM, pltpu.HBM, pl.ANY
DMA = pltpu.SemaphoreType.DMA
copy = pltpu.make_async_copy


def three_parts(x):
    high = x.astype(BF16).astype(F32)
    rest = x - high
    mid = rest.astype(BF16).astype(F32)
    return [high, mid, (rest - mid).astype(BF16).astype(F32)]


def stacked(parts, rows):
    which = lax.broadcasted_iota(I32, (rows, parts[0].shape[1]), 0)
    tile = jnp.zeros(which.shape, F32)
    for at, part in enumerate(parts):
        tile = jnp.where(which == at, jnp.broadcast_to(part, which.shape), tile)
    return tile


def entries(values, first, half, rb):
    ra = values.shape[0]
    one = [values[m : m + 1, first : first + half] for m in range(ra)]
    return jnp.concatenate(one * rb, axis=1)


class Sizes:
    def __init__(self, half, ra, rb, bs):
        self.half, self.ra, self.rb, self.bs = half, ra, rb, bs
        self.wide = ra * bs
        self.tiles = JW * bs // LANES

    def message(self):
        return VMEM((self.half * self.wide + META, self.rb * self.bs), BF16)

    def window(self):
        return VMEM((self.half, self.tiles, self.bs, LANES), F32)


class In:
    def __init__(self, array, place):
        self.array, self.place = array, place
        if place in (VMEM, HBM):
            self.array = pltpu.with_memory_space_constraint(array, place)


def kernel_call(name, body, ins, outs, aliases=(), scratch=None):
    names = list(ins) + list(outs) + list(scratch or {})

    def kernel(*refs):
        body(types.SimpleNamespace(**dict(zip(names, refs))))

    def out_place(shape):
        return ANY if isinstance(shape, jax.ShapeDtypeStruct) else VMEM

    got = pl.pallas_call(
        kernel,
        out_shape=list(outs.values()),
        in_specs=[pl.BlockSpec(memory_space=one.place) for one in ins.values()],
        out_specs=[pl.BlockSpec(memory_space=out_place(shape)) for shape in outs.values()],
        input_output_aliases={list(ins).index(a): list(outs).index(b) for a, b in aliases},
        scratch_shapes=list((scratch or {}).values()),
        compiler_params=pltpu.CompilerParams(vmem_limit_bytes=VMEM_LIMIT),
        cost_estimate=pl.CostEstimate(flops=2 * 10**10, bytes_accessed=1024, transcendentals=0),
        name=name,
    )(*[one.array for one in ins.values()])
    return types.SimpleNamespace(**dict(zip(outs, got)))


class Gather:
    def __init__(self, z, refs, message, flip, which, sem):
        self.z, self.refs, self.message, self.flip, self.which, self.sem = z, refs, message, flip, which, sem

    def start(self):
        z, refs = self.z, self.refs
        cols = refs.cols_s.at[self.which]
        base = (refs.info[0] ^ self.flip) * z.half

        def one_row(i, _):
            for m in range(z.ra):
                at = pl.multiple_of((i * z.ra + m) * z.bs, z.bs)
                copy(refs.b.at[cols[m, base + i]], self.message.at[pl.ds(at, z.bs)], self.sem).start()
            return 0

        lax.fori_loop(0, z.half, one_row, 0, unroll=2)

    def finish(self):
        z, refs = self.z, self.refs
        table, cols = refs.table, refs.cols_v[self.which]
        kw = table.shape[1]
        both = [entries(cols, h * z.half, z.half, z.rb) for h in range(2)]
        named = jnp.where((refs.info[0] ^ self.flip) == 1, both[1], both[0])
        named = jnp.broadcast_to(named, (kw, named.shape[1]))
        picked = lax.broadcasted_iota(I32, named.shape, 0) == named
        picked = jnp.where(picked, 1.0, 0.0).astype(BF16)
        found = jnp.dot(table[...], picked, preferred_element_type=F32)
        slot = lax.broadcasted_iota(I32, (1, found.shape[1]), 1) // (z.ra * z.half)
        parts = []
        for part in range(PARTS):
            value = found[part * z.rb : part * z.rb + 1]
            for n in range(1, z.rb):
                value = jnp.where(slot == n, found[part * z.rb + n : part * z.rb + n + 1], value)
            parts.append(value)
        size = z.half * z.wide
        self.message[pl.ds(size, META), :] = stacked(parts, META).astype(BF16)
        blocks = self.message.at[pl.ds(0, size)]
        copy(blocks, blocks, self.sem).wait()


def add_scratch(z, count=1):
    return dict(
        prods=VMEM((count, z.half * z.wide, LANES), F32),
        scl_v=VMEM((8, LANES), F32),
        col_v=VMEM((8, LANES), I32),
        scl_s=SMEM((8, LANES), F32),
        col_s=SMEM((8, LANES), I32),
        add_sems=DMA((2,)),
    )


class Add:
    def __init__(self, z, refs, pairs):
        self.z, self.refs, self.pairs = z, refs, pairs

    def start(self):
        z, refs = self.z, self.refs
        for at, (a, b) in enumerate(self.pairs):
            a_meta = a[pl.ds(a.shape[0] - META, META), :].astype(F32)
            b_meta = b[pl.ds(b.shape[0] - META, META), :].astype(F32)
            scl_a = a_meta[0:1] + a_meta[1:2] + a_meta[2:3]
            scl_b = b_meta[0:1] + b_meta[1:2] + b_meta[2:3]
            refs.scl_v[at : at + 1, :] = scl_a * scl_b
            refs.col_v[at : at + 1, :] = (b_meta[3:4] * 256.0 + b_meta[4:5]).astype(I32)
        self.moves = [
            copy(refs.scl_v, refs.scl_s, refs.add_sems.at[0]),
            copy(refs.col_v, refs.col_s, refs.add_sems.at[1]),
        ]
        for move in self.moves:
            move.start()
        row_block = lax.broadcasted_iota(I32, (z.wide, z.wide), 0) // z.bs
        col_block = lax.broadcasted_iota(I32, (z.wide, z.wide), 1) // z.bs
        diagonal = jnp.where(row_block == col_block, 1.0, 0.0).astype(BF16)
        for at, (a, b) in enumerate(self.pairs):
            for i in range(z.half):
                left = a[pl.ds(i * z.bs, z.bs), :]
                left = jnp.concatenate([left] * z.ra, axis=0) * diagonal
                rows = pl.ds(i * z.wide, z.wide)
                refs.prods[at, rows, :] = jnp.dot(left, b[rows, :], preferred_element_type=F32)

    def finish(self, after_row=None):
        z, refs, acc = self.z, self.refs, self.refs.acc
        per = LANES // z.bs
        for move in self.moves:
            move.wait()
        lane_block = lax.broadcasted_iota(I32, (8, LANES), 1) // z.bs
        for i in range(z.half):
            for at in range(len(self.pairs)):
                for m in range(z.ra):
                    value = refs.prods[at, pl.ds((i * z.ra + m) * z.bs, z.bs), :]
                    placed = []
                    for n in range(z.rb):
                        entry = (n * z.ra + m) * z.half + i
                        column = refs.col_s[at, entry]
                        place = column & (per - 1)
                        moved = pltpu.roll(value, ((place - n) & (per - 1)) * z.bs, 1)
                        scale = jnp.where(lane_block == place, refs.scl_s[at, entry], 0.0)
                        placed.append((column // per, moved * jnp.concatenate([scale] * (z.bs // 8), axis=0)))
                    for tile, moved in placed:
                        acc[i, tile] = acc[i, tile] + moved
            if after_row is not None:
                after_row(i)


def clear(acc):
    for i in range(acc.shape[0]):

        def clear_tile(tile, _, i=i):
            acc[i, tile] = jnp.zeros(acc.shape[2:], F32)
            return 0

        lax.fori_loop(0, acc.shape[1], clear_tile, 0, unroll=8)


class WriteAll:
    def __init__(self, z, refs):
        self.z, self.refs, self.sent = z, refs, []

    @staticmethod
    def scratch(z):
        return dict(stage=VMEM((SLOTS, z.bs, JW * z.bs // CHUNKS), BF16), out_sems=DMA((SLOTS,)))

    def send(self, at):
        i, chunk = self.sent[at]
        slot, width = at % SLOTS, self.refs.stage.shape[2]
        there = self.refs.out.at[i, :, pl.ds(chunk * width, width)]
        return copy(self.refs.stage.at[slot], there, self.refs.out_sems.at[slot])

    def row(self, i):
        acc, stage = self.refs.acc, self.refs.stage
        tiles = self.z.tiles // CHUNKS
        for chunk in range(CHUNKS):
            at = len(self.sent)
            if at >= SLOTS:
                self.send(at - SLOTS).wait()
            for tile in range(tiles):
                piece = acc[i, chunk * tiles + tile].astype(BF16)
                stage[at % SLOTS, :, pl.ds(tile * LANES, LANES)] = piece
            self.sent.append((i, chunk))
            self.send(at).start()

    def finish(self):
        for at in range(max(0, len(self.sent) - SLOTS), len(self.sent)):
            self.send(at).wait()


def prepare(info, own_cols, b_scl, b_pos):
    rb, kw = b_scl.shape

    def body(refs):
        moves = [
            copy(refs.b_scl, refs.scl, refs.sems.at[0]),
            copy(refs.b_pos, refs.pos, refs.sems.at[1]),
            copy(refs.own_cols, refs.own, refs.sems.at[2]),
        ]
        for move in moves:
            move.start()
        for move in moves:
            move.wait()
        scale, column = refs.scl[...], refs.pos[...]
        table = three_parts(scale) + [(column >> 8).astype(F32), (column & 255).astype(F32)]
        table.append(jnp.zeros((refs.table.shape[0] - PARTS * rb, kw), F32))
        refs.table[...] = jnp.concatenate(table, axis=0).astype(BF16)

    return kernel_call(
        "prepare",
        body,
        dict(info=In(info, SMEM), own_cols=In(own_cols, HBM), b_scl=In(b_scl, HBM), b_pos=In(b_pos, HBM)),
        dict(table=VMEM((-(-PARTS * rb // 16) * 16, kw), BF16), own=VMEM(own_cols.shape, I32)),
        scratch=dict(scl=VMEM(b_scl.shape, F32), pos=VMEM(b_pos.shape, I32), sems=DMA((3,))),
    )


def split(z, info, a, a_scl, after, asked):
    def body(refs):
        scale = refs.a_scl[...]
        both = [entries(scale, h * z.half, z.half, z.rb) for h in range(2)]
        size = z.half * z.bs
        for flip, out in enumerate((refs.kept, refs.given)):
            side = refs.info[0] ^ flip
            out[0, pl.ds(0, size), :] = refs.a[pl.ds(pl.multiple_of(side * size, size), size), :]
            parts = three_parts(jnp.where(side == 1, both[1], both[0]))
            out[0, pl.ds(size, META), :] = stacked(parts, META).astype(BF16)

    piece = VMEM((1, z.half * z.bs + META, z.wide), BF16)
    return kernel_call(
        "split",
        body,
        dict(
            info=In(info, SMEM), a=In(a, VMEM), a_scl=In(a_scl, VMEM), after=In(after, ANY), asked=In(asked, ANY)
        ),
        dict(kept=piece, given=piece),
    )


def join(own, taken):
    count = own.shape[0]

    def body(refs):
        refs.both[pl.ds(0, count)] = refs.own[...]
        refs.both[pl.ds(count, count)] = refs.taken[...]

    outs = dict(both=VMEM((2 * count,) + own.shape[1:], own.dtype))
    return kernel_call("join", body, dict(own=In(own, VMEM), taken=In(taken, VMEM)), outs).both


def answer(z, info, cols, which, flips, table, b, after):
    outs = {"m" + str(flip): z.message() for flip in flips}

    def body(refs):
        gathers = [
            Gather(z, refs, getattr(refs, name), flip, which, refs.sems.at[flip]) for name, flip in zip(outs, flips)
        ]
        for gather in gathers:
            gather.start()
        for gather in gathers:
            gather.finish()

    return kernel_call(
        "answer",
        body,
        dict(
            info=In(info, SMEM),
            cols_s=In(cols, SMEM),
            cols_v=In(cols, VMEM),
            table=In(table, VMEM),
            b=In(b, HBM),
            after=In(after, ANY),
        ),
        outs,
        scratch=dict(sems=DMA((2,))),
    )


def own_blocks(z, info, cols, table, b, kept, after):
    def body(refs):
        answer = Gather(z, refs, refs.message, 1, 0, refs.sems.at[0])
        local = Gather(z, refs, refs.local, 0, 0, refs.sems.at[1])
        local.start()
        answer.start()
        clear(refs.acc)
        local.finish()
        add = Add(z, refs, [(refs.kept.at[0], refs.local)])
        add.start()
        answer.finish()
        add.finish()

    return kernel_call(
        "own_blocks",
        body,
        dict(
            info=In(info, SMEM),
            cols_s=In(cols, SMEM),
            cols_v=In(cols, VMEM),
            table=In(table, VMEM),
            b=In(b, HBM),
            kept=In(kept, VMEM),
            after=In(after, ANY),
        ),
        dict(acc=z.window(), message=z.message()),
        scratch=dict(sems=DMA((2,)), local=z.message(), **add_scratch(z)),
    )


def add_messages(z, info, left, arrived, acc, answer=None, after=None, write=False):
    ins = dict(info=In(info, SMEM), left=In(left, VMEM), acc_in=In(acc, VMEM))
    taken = {"m" + str(at): In(message, VMEM) for at, (_, _, message) in enumerate(arrived)}
    ins.update(taken)
    outs = dict(acc=z.window())
    aliases = [("acc_in", "acc")]
    scratch = add_scratch(z, len(arrived))
    if answer is not None:
        cols, which, side, table, b = answer
        ins.update(cols_s=In(cols, SMEM), cols_v=In(cols, VMEM), table=In(table, VMEM), b=In(b, HBM))
        outs.update(message=z.message())
        scratch.update(sems=DMA((1,)))
    if after is not None:
        ins.update(after=In(after, ANY))
    if write:
        outs.update(out=jax.ShapeDtypeStruct((z.half, z.bs, JW * z.bs), BF16))
        scratch.update(WriteAll.scratch(z))

    def body(refs):
        if answer is not None:
            gather = Gather(z, refs, refs.message, side, which, refs.sems.at[0])
            gather.start()
        pairs = []
        for name, (by, flip, _) in zip(taken, arrived):
            place = flip if by == 0 else refs.info[1 + by] * 2 + flip
            pairs.append((refs.left.at[place], getattr(refs, name)))
        add = Add(z, refs, pairs)
        add.start()
        if answer is not None:
            gather.finish()
        if write:
            writer = WriteAll(z, refs)
            add.finish(writer.row)
            writer.finish()
        else:
            add.finish()

    return kernel_call("add_messages", body, ins, outs, aliases, scratch)


def on_device(a_blocks, a_scale, a_cols, b_blocks, b_scale, b_cols):
    panels = lax.axis_size(ROW)
    columns = lax.axis_size(COL)
    halves = columns // panels
    a_part, a_scl, a_pos = a_blocks[0, 0], a_scale[0, 0].T, a_cols[0, 0].T
    b_part = b_blocks[0, 0]
    b_scl, b_pos = b_scale[0, 0].T, b_cols[0, 0].T
    nrows, bs, _ = a_part.shape
    z = Sizes(nrows // halves, a_scl.shape[0], b_scl.shape[0], bs)
    row = lax.axis_index(ROW)
    parity = lax.axis_index(COL) % halves
    info = jnp.stack([parity] + [row ^ ((row - by) % panels) for by in range(panels)]).astype(I32)

    def step(value, by, flip):
        pairs = [
            (c, ((c // halves + by) % panels) * halves + (c % halves ^ flip)) for c in range(columns)
        ]
        return lax.ppermute(value, COL, pairs)

    def named_by(by, cols):
        pairs = []
        for r in range(panels):
            for c in range(columns):
                to_row = (r + by) % panels
                to_col = (c - halves * by) % columns
                pairs.append((r * columns + c, to_row * columns + to_col))
        return lax.ppermute(cols, (ROW, COL), pairs)

    order = sorted(range(1, panels), key=lambda by: -min(by, panels - by))
    last = order[-1]
    own_cols = a_pos[None]

    first_cols = named_by(order[0], own_cols)
    ready = prepare(info, own_cols, b_scl, b_pos)
    own_cols, table = ready.own, ready.table
    cols = join(own_cols, first_cols)
    asked, known, by = {0: (own_cols, 0)}, [0, order[0]], panels // 4
    more_cols = named_by(by, cols)
    got = answer(z, info, cols, 1, (0, 1), table, b_part, table)
    after = got.m0
    moving = {(order[0], flip): step(one, order[0], flip) for flip, one in enumerate((got.m0, got.m1))}
    pieces = split(z, info, a_part.reshape(nrows * bs, z.wide), a_scl, after, more_cols)
    while True:
        asked.update({(to + by) % panels: (more_cols, at) for at, to in enumerate(known)})
        known += [(to + by) % panels for to in known]
        by //= 2
        if not by:
            break
        cols = join(cols, more_cols)
        more_cols = named_by(by, cols)

    own_left = join(pieces.kept, step(pieces.given, 0, 1))
    left = own_left
    bit = 1
    while bit < panels:
        left = join(left, lax.ppermute(left, ROW, [(r, r ^ bit) for r in range(panels)]))
        bit *= 2

    for by in order[1:-1]:
        for flip in range(halves):
            got = answer(z, info, *asked[by], (flip,), table, b_part, after)
            (after,) = vars(got).values()
            moving[by, flip] = step(after, by, flip)
    mine = own_blocks(z, info, own_cols, table, b_part, pieces.kept, after)
    taken = step(mine.message, 0, 1)

    got = add_messages(
        z, info, own_left, [(0, 1, taken)], mine.acc, (*asked[last], 0, table, b_part)
    )
    acc, ends = got.acc, [got.message]
    ends.append(answer(z, info, *asked[last], (1,), table, b_part, ends[0]).m1)
    early = [(by, flip) for by in order[:-1] for flip in range(halves)]
    early[:halves] = early[halves - 1 :: -1]
    after = ends[1]
    for by, flip in early[:-1]:
        acc = add_messages(z, info, left, [(by, flip, moving[by, flip])], acc, after=after).acc
        after = None
    both = [(*early[-1], moving[early[-1]]), (last, 0, step(ends[0], last, 0))]
    acc = add_messages(z, info, left, both, acc).acc
    out = add_messages(z, info, left, [(last, 1, step(ends[1], last, 1))], acc, write=True).out
    return out[None, None]


def solution(mesh):
    in_specs = (
        P(COL, ROW, None, None, None),
        P(COL, ROW, None, None),
        P(COL, ROW, None, None),
        P(COL, ROW, None, None, None),
        P(COL, ROW, None, None),
        P(COL, ROW, None, None),
    )
    out_specs = P(COL, ROW, None, None, None)
    return jax.shard_map(
        on_device, mesh=mesh, in_specs=in_specs, out_specs=out_specs, check_vma=False
    )
```
